32 devices in a mesh: dp: 4 (over y, x), row: 4 (over z), col: 2 (over core).
Axes of the slice: x: 2, y: 2, z: 4, core: 2. Of those that a mesh axis runs over, the one named last changes fastest.
Arguments:
- tokens: bfloat16 [1088, 4096], P('row', ('dp', 'col')), may hold values from -6 to 6
- block_order: int32 [4, 16], P('dp'), may hold values from 0 to 15, each once within a row
- first_gain: float32 [1088], P('row'), may hold values from 0.25 to 1.75
- first_shift: float32 [1088], P('row'), may hold values from -4 to 4
- qkv_weight: bfloat16 [1088, 3264], P('row', 'col'), may hold values from -0.1875 to 0.1875
- query_value_bias: float32 [2, 1088], replicated, may hold values from -4 to 4
- output_weight: bfloat16 [1088, 1088], P('col', 'row'), may hold values from -0.5 to 0.5
- output_bias: float32 [1088], P('row'), may hold values from -4 to 4
- second_gain: float32 [1088], P('row'), may hold values from 0.25 to 1.75
- second_shift: float32 [1088], P('row'), may hold values from -4 to 4
- up_weight: bfloat16 [1088, 4352], P('row', 'col'), may hold values from -0.1875 to 0.1875
- up_bias: float32 [4352], P('col'), may hold values from -4 to 4
- down_weight: bfloat16 [1088, 4352], P('row', 'col'), may hold values from -0.09375 to 0.09375
- down_bias: float32 [1088], P('row'), may hold values from -4 to 4
- cotangent: bfloat16 [1088, 4096], P('row', ('dp', 'col')), may hold values from -6 to 6
Outputs:
- result: bfloat16 [1088, 4096], P('row', ('dp', 'col'))
- input_grad: float32 [1088, 4096], P('row', ('dp', 'col'))
- first_gain_grad: float32 [1088], replicated
- first_shift_grad: float32 [1088], replicated
- qkv_weight_grad: float32 [1088, 3264], P('row', 'col')
- query_value_bias_grad: float32 [2, 1088], replicated
- output_weight_grad: float32 [1088, 1088], P('col', 'row')
- output_bias_grad: float32 [1088], replicated
- second_gain_grad: float32 [1088], replicated
- second_shift_grad: float32 [1088], replicated
- up_weight_grad: float32 [1088, 4352], P('row', 'col')
- up_bias_grad: float32 [4352], replicated
- down_weight_grad: float32 [1088, 4352], P('row', 'col')
- down_bias_grad: float32 [1088], replicated
The draws below stay inside these ranges and needn't reach their ends.
Inputs may be any that keep to these rules, and one draw needn't show every extreme that they name: Each row names every position block once: stored block b of a sequence holds that sequence's positions block_order[s, b] * 64 to block_order[s, b] * 64 + 63.
All inputs are finite; a program needn't handle non-finite values.
Results may differ from the reference program's by a relative error of at most 0.011.
Values may be sent and summed in bfloat16 or wider, within the bound.
No kernel may reach another device: no remote copies, remote signals or barrier semaphores. Data moves between devices by JAX's collectives and lax.ppermute only.
A program may use at most 320 MiB of HBM per device.

```python
import jax
import jax.numpy as jnp
from jax import lax

D = 1088
HEADS = 17
HEAD_DIM = 64
FF = 4352
LEN = 1024
NBLK = 16
BLK = 64
NSEQ = 4
TOKENS = 4096


def block_scale(rng, shape, shards, least, largest):
    def one(dim, shards_of):
        heights = jax.random.uniform(jax.random.fold_in(jax.random.fold_in(rng, 6), dim), (shards_of,), jnp.float32, least / len(shards), largest / len(shards))
        return jnp.repeat(jnp.exp(heights), shape[dim] // shards_of).reshape((-1,) + (1,) * (len(shape) - dim - 1))

    loudness = one(*shards[0])
    for cut in shards[1:]:
        loudness = loudness * one(*cut)
    return loudness


def centred(rng, dims, scale, reach, split=(), kind=jnp.bfloat16):
    factor_of = block_scale(rng, dims, split, -0.22, 0.18) if split else 1.0
    entries = jax.random.normal(rng, dims, jnp.float32) * scale * factor_of
    return jnp.minimum(jnp.maximum(entries, -reach), reach).astype(kind)


def setup_inputs(seed: int = 0) -> dict:
    arg_keys = jax.random.split(jax.random.key(seed), 16)
    tokens = centred(arg_keys[0], (D, TOKENS), 1.0, 6.0, ((0, 4), (1, 8)))
    block_order = jax.vmap(lambda own: jax.random.permutation(own, NBLK))(jax.random.split(arg_keys[1], NSEQ)).reshape((NSEQ, NBLK)).astype(jnp.int32)
    first_gain = jnp.clip(1.0 + 0.15 * jax.random.normal(arg_keys[2], (D,), jnp.float32), 0.25, 1.75)
    first_shift = centred(arg_keys[3], (D,), 0.3, 4.0, ((0, 4),), jnp.float32)
    qkv_weight = centred(arg_keys[4], (D, 3 * D), D ** -0.5, 0.1875, ((0, 4), (1, 2)))
    query_value_bias = centred(arg_keys[5], (2, D), 0.3, 4.0, (), jnp.float32)
    output_weight = centred(arg_keys[6], (D, D), (D // 8) ** -0.5, 0.5, ((0, 2), (1, 4)))
    output_bias = centred(arg_keys[7], (D,), 0.3, 4.0, ((0, 4),), jnp.float32)
    second_gain = jnp.clip(1.0 + 0.15 * jax.random.normal(arg_keys[8], (D,), jnp.float32), 0.25, 1.75)
    second_shift = centred(arg_keys[9], (D,), 0.3, 4.0, ((0, 4),), jnp.float32)
    up_weight = centred(arg_keys[10], (D, FF), D ** -0.5, 0.1875, ((0, 4), (1, 2)))
    up_bias = centred(arg_keys[11], (FF,), 0.3, 4.0, ((0, 2),), jnp.float32)
    down_weight = centred(arg_keys[12], (D, FF), FF ** -0.5, 0.09375, ((0, 4), (1, 2)))
    down_bias = centred(arg_keys[13], (D,), 0.3, 4.0, ((0, 4),), jnp.float32)
    cotangent = centred(arg_keys[14], (D, TOKENS), 1.0, 6.0, ((0, 4), (1, 8)))
    return {"tokens": tokens, "block_order": block_order, "first_gain": first_gain, "first_shift": first_shift, "qkv_weight": qkv_weight, "query_value_bias": query_value_bias, "output_weight": output_weight, "output_bias": output_bias, "second_gain": second_gain, "second_shift": second_shift, "up_weight": up_weight, "up_bias": up_bias, "down_weight": down_weight, "down_bias": down_bias, "cotangent": cotangent}


highest = lax.Precision.HIGHEST
epsilon = 1e-05

@jax.custom_vjp
def low(v):
    return lax.optimization_barrier(v.astype(jnp.bfloat16)).astype(jnp.float32)

@jax.custom_vjp
def low_back(v):
    return v

def low_keep(v):
    return (low(v), None)

def low_pass(kept, grad):
    return (grad,)

def back_keep(v):
    return (v, None)

def back_low(kept, grad):
    return (low(grad),)
low.defvjp(low_keep, low_pass)
low_back.defvjp(back_keep, back_low)

def product(left_side, right_side):
    return jnp.dot(left_side, right_side, precision=highest)

def normalize(hidden, norm_gain, norm_shift):
    centered = hidden - lax.optimization_barrier(jnp.mean(hidden, axis=1, keepdims=True))
    variance = lax.optimization_barrier(jnp.mean(centered * centered, axis=1, keepdims=True))
    return centered * lax.rsqrt(variance + epsilon) * norm_gain + norm_shift

def block_forward(inputs, order_row, weights):
    first_gain, first_shift, qkv_weight, query_value_bias, output_weight, output_bias, second_gain, second_shift, up_weight, up_bias, down_weight, down_bias = weights
    first_normed = low(normalize(inputs, first_gain, first_shift))
    bias_row = jnp.concatenate([query_value_bias[0], jnp.zeros_like(query_value_bias[0]), query_value_bias[1]])
    projected = low_back(low(product(first_normed, qkv_weight) + bias_row))
    queries = projected[:, :D].reshape(LEN, HEADS, HEAD_DIM)
    keys_all = projected[:, D:2 * D].reshape(LEN, HEADS, HEAD_DIM)
    values_all = projected[:, 2 * D:].reshape(LEN, HEADS, HEAD_DIM)
    scores = low_back(jnp.einsum('qhd,khd->hqk', queries, keys_all, precision=highest) * HEAD_DIM ** (-0.5))
    offsets = jnp.arange(BLK, dtype=jnp.int32)
    places = (order_row[:, None] * BLK + offsets[None, :]).reshape(LEN)
    allowed = places[None, :] <= places[:, None]
    scores = jnp.where(allowed[None], scores, -1e+30)
    attention_weights = low(jax.nn.softmax(scores, axis=-1))
    attended = jnp.einsum('hqk,khd->qhd', attention_weights, values_all, precision=highest).reshape(LEN, D)
    attended = low_back(low(attended))
    middle = inputs + low_back(product(attended, output_weight) + output_bias)
    second_normed = low(normalize(middle, second_gain, second_shift))
    before = low_back(product(second_normed, up_weight) + up_bias)
    hidden = low(jax.nn.gelu(before, approximate=False))
    return middle + low_back(product(hidden, down_weight.T) + down_bias)

def reference(tokens, block_order, first_gain, first_shift, qkv_weight, query_value_bias, output_weight, output_bias, second_gain, second_shift, up_weight, up_bias, down_weight, down_bias, cotangent):
    params = tuple((member.astype(jnp.float32) for member in (first_gain, first_shift, qkv_weight, query_value_bias, output_weight, output_bias, second_gain, second_shift, up_weight, up_bias, down_weight, down_bias)))
    sequences = tokens.astype(jnp.float32).T.reshape(NSEQ, LEN, D)
    upstream = cotangent.astype(jnp.float32).T.reshape(NSEQ, LEN, D)

    def one_sequence(running, carried):
        seq_rows, order_row, grad_rows = carried

        def forward(layer_input, *weights):
            return block_forward(layer_input, order_row, weights)
        output, pullback = jax.vjp(forward, seq_rows, *params)
        gradients = pullback(grad_rows)
        running = tuple((running_sum + gradient for running_sum, gradient in zip(running, gradients[1:])))
        return (running, (output, gradients[0]))
    zeros_tuple = tuple((jnp.zeros_like(member) for member in params))
    summed, (outputs, input_grads) = lax.scan(one_sequence, zeros_tuple, (sequences, block_order, upstream))
    return (outputs.reshape(TOKENS, D).T.astype(jnp.bfloat16), input_grads.reshape(TOKENS, D).T, summed[0], summed[1], summed[2], summed[3], summed[4], summed[5], summed[6], summed[7], summed[8], summed[9], summed[10], summed[11])
```

```python
import jax
import jax.numpy as jnp
from jax import lax
from jax.sharding import PartitionSpec as P

D = 1088
HEADS = 17
HEAD_DIM = 64
FF = 4352
epsilon = 1e-05
f32 = jnp.float32
bf16 = jnp.bfloat16


def gelu_exact(before):
    return jax.nn.gelu(before, approximate=False)


def dot(left, right, left_dim, right_dim):
    return lax.dot_general(
        left, right, (((left_dim,), (right_dim,)), ((), ())), preferred_element_type=f32
    )


def swap(values, axis, k):
    return lax.ppermute(values, axis, [(i, i ^ k) for i in range(lax.axis_size(axis))])


def spread(values, axis):
    return [values] + [swap(values, axis, k) for k in range(1, lax.axis_size(axis))]


def trade(pieces, axis):
    return [pieces[0]] + [swap(pieces[k], axis, k) for k in range(1, len(pieces))]


def settle(pieces, index):
    pieces = list(pieces)
    bit = 1
    while bit < len(pieces):
        odd = (index & bit) != 0
        pieces = [jnp.where(odd, pieces[k ^ bit], pieces[k]) for k in range(len(pieces))]
        bit *= 2
    return pieces


def total(pieces):
    out = pieces[0].astype(f32)
    for piece in pieces[1:]:
        out = out + piece.astype(f32)
    return out


def cut(values, start, size, dim):
    return lax.dynamic_slice_in_dim(values, start, size, dim)


def norm_forward(rows, gain, shift):
    average = jnp.sum(rows, 0, keepdims=True) / D
    centered = rows - average
    variance = jnp.sum(centered * centered, 0, keepdims=True) / D
    inverse = lax.rsqrt(variance + epsilon)
    normal = centered * inverse
    return (normal * gain + shift).astype(bf16), normal, inverse


def norm_backward(upstream, normal, inverse, gain):
    scaled = upstream * gain
    first = jnp.sum(scaled, 0, keepdims=True) / D
    second = jnp.sum(scaled * normal, 0, keepdims=True) / D
    return inverse * (scaled - first - normal * second)


def attend(queries, keys, values, allowed):
    scores = jnp.einsum("hdk,hdq->hkq", keys, queries, preferred_element_type=f32)
    scores = jnp.where(allowed[None], scores * HEAD_DIM ** (-0.5), -1e30)
    powers = jnp.exp(scores - jnp.max(scores, 1, keepdims=True))
    probability = powers / jnp.sum(powers, 1, keepdims=True)
    out = jnp.einsum(
        "hdk,hkq->hdq", values, probability.astype(bf16), preferred_element_type=f32
    ).astype(bf16)
    return probability, out


def attend_back(queries, keys, values, probability, grad_out):
    scale = HEAD_DIM ** (-0.5)
    grad_weights = jnp.einsum("hdk,hdq->hkq", values, grad_out, preferred_element_type=f32)
    inner = jnp.sum(probability * grad_weights, 1, keepdims=True)
    grad_scores = (probability * (grad_weights - inner)).astype(bf16)
    grad_q = jnp.einsum("hdk,hkq->hdq", keys, grad_scores, preferred_element_type=f32) * scale
    grad_k = jnp.einsum("hdq,hkq->hdk", queries, grad_scores, preferred_element_type=f32) * scale
    grad_v = jnp.einsum(
        "hdq,hkq->hdk", grad_out, probability.astype(bf16), preferred_element_type=f32
    )
    return grad_q, grad_k, grad_v


def shards(
    tokens,
    block_order,
    first_gain,
    first_shift,
    qkv_weight,
    query_value_bias,
    output_weight,
    output_bias,
    second_gain,
    second_shift,
    up_weight,
    up_bias,
    down_weight,
    down_bias,
    cotangent,
):
    R, G = lax.axis_size("row"), lax.axis_size("dp")
    r, c, g = lax.axis_index("row"), lax.axis_index("col"), lax.axis_index("dp")
    low = c == 0
    db, T = tokens.shape
    tq = T // R
    hp = HEADS // R
    W = hp * HEAD_DIM
    E = HEADS * HEAD_DIM - W * R
    X = E // HEAD_DIM
    half = W // 2
    pw = max(half, 2 * E)
    sub = up_weight.shape[1] // R
    GH = G // 2
    hr = db // GH

    def pad(values):
        return jnp.pad(values, ((0, 0), (0, pw - values.shape[1])))

    x = jnp.concatenate(spread(tokens, "row"), 0).astype(f32)
    vectors = jnp.concatenate(
        spread(
            jnp.stack([first_gain, first_shift, output_bias, second_gain, second_shift]), "row"
        ),
        1,
    )
    g1, s1, ob, g2, s2 = [vectors[i][:, None] for i in range(5)]

    side = qkv_weight.shape[1] - D
    own_part = cut(qkv_weight, c * side, D, 1)
    own_keys = cut(qkv_weight, (1 - c) * D, side, 1)
    other_keys = swap(own_keys, "col", 1)
    key_part = jnp.concatenate(
        [jnp.where(low, own_keys, other_keys), jnp.where(low, other_keys, own_keys)], 1
    )
    source = jnp.where(g == 3, key_part, own_part)
    extras = pad(jnp.concatenate([own_part[:, R * W :], key_part[:, R * W :]], 1))
    offset = jnp.where(g == 3, c, g & 1) * half
    chunks = [
        jnp.where(g == 2, extras, pad(cut(source, (r ^ k) * W + offset, half, 1)))
        for k in range(R)
    ]
    piece = jnp.concatenate(trade(chunks, "row"), 0)
    own_w = jnp.concatenate(settle(spread(piece, "dp"), g), 1)
    other_w = swap(own_w, "col", 1)
    lo, hi = jnp.where(low, own_w, other_w), jnp.where(low, other_w, own_w)
    ex = 2 * pw
    kk = 3 * pw
    wqkv = jnp.concatenate(
        [
            lo[:, :half],
            lo[:, pw : pw + half],
            lo[:, ex : ex + E],
            lo[:, kk : kk + half],
            hi[:, kk : kk + half],
            lo[:, ex + E : ex + 2 * E],
            hi[:, :half],
            hi[:, pw : pw + half],
            hi[:, ex : ex + E],
        ],
        1,
    )
    HW = W + E
    bias = jnp.concatenate(
        [
            cut(query_value_bias[0], r * W, W, 0),
            query_value_bias[0, R * W :],
            jnp.zeros((HW,), f32),
            cut(query_value_bias[1], r * W, W, 0),
            query_value_bias[1, R * W :],
        ]
    )[:, None]

    part = cut(output_weight, g * (output_weight.shape[0] // G), output_weight.shape[0] // G, 0)
    part = jnp.concatenate(spread(part, "row"), 1)
    own_o = jnp.concatenate(settle(spread(part, "dp"), g), 0)
    other_o = swap(own_o, "col", 1)
    wo = jnp.concatenate([jnp.where(low, own_o, other_o), jnp.where(low, other_o, own_o)], 0)

    part = jnp.where(
        g < GH,
        cut(up_weight, (g % GH) * hr, hr, 0),
        cut(down_weight, (g % GH) * hr, hr, 0),
    )
    part = jnp.stack(trade([cut(part, (r ^ k) * sub, sub, 1) for k in range(R)], "row"))
    own_f = settle(spread(part, "dp"), g)
    own_f = jnp.stack(
        [
            jnp.stack(own_f[:GH], 1).reshape(D, sub),
            jnp.stack(own_f[GH:], 1).reshape(D, sub),
        ]
    )
    wf = jnp.concatenate([own_f, swap(own_f, "col", 1)], 2)
    wup, wdn = wf[0], wf[1]
    own_ub = cut(up_bias, r * sub, sub, 0)
    ub = jnp.concatenate([own_ub, swap(own_ub, "col", 1)])[:, None]

    block = T * 2 // block_order.shape[1]
    places = (
        block_order.reshape(-1)[:, None] * block + jnp.arange(block, dtype=jnp.int32)[None, :]
    ).reshape(-1)
    own_places = cut(places, c * T, T, 0)
    key_places = jnp.concatenate([own_places, cut(places, (1 - c) * T, T, 0)])
    allowed = key_places[:, None] <= own_places[None, :]
    extra_allowed = cut(allowed, r * tq, tq, 1)

    normed1, n1, inv1 = norm_forward(x, g1, s1)
    projected = (dot(wqkv, normed1, 0, 0) + bias).astype(bf16)
    own_kv = projected[HW:]
    kv = jnp.concatenate([own_kv, swap(own_kv, "col", 1)], 1)
    S = 2 * T
    queries = projected[:W].reshape(hp, HEAD_DIM, T)
    keys = kv[:W].reshape(hp, HEAD_DIM, S)
    values = kv[HW : HW + W].reshape(hp, HEAD_DIM, S)
    qx = cut(projected[W:HW], r * tq, tq, 1).reshape(X, HEAD_DIM, tq)
    kx = kv[W:HW].reshape(X, HEAD_DIM, S)
    vx = kv[HW + W :].reshape(X, HEAD_DIM, S)
    prob, out = attend(queries, keys, values, allowed)
    probx, outx = attend(qx, kx, vx, extra_allowed)
    packed = jnp.concatenate([out.reshape(W, T), outx.reshape(E // R, T)], 0)
    rows = settle(spread(packed, "row"), r)
    attended = jnp.concatenate(
        [piece[:W] for piece in rows]
        + [jnp.concatenate([piece[W:].reshape(E, tq) for piece in rows], 1)],
        0,
    )
    middle = x + dot(wo, attended, 0, 0) + ob
    normed2, n2, inv2 = norm_forward(middle, g2, s2)

    before = dot(wup, normed2, 0, 0) + ub
    hidden = gelu_exact(before).astype(bf16)
    down = dot(wdn, hidden, 1, 0)
    down = total([down[:db]] + trade(list(down.astype(bf16).reshape(R, db, T)), "row")[1:])
    result = (middle[:db] + down + down_bias[:, None]).astype(bf16)

    upstream = jnp.concatenate(spread(cotangent, "row"), 0)
    grad_hidden = dot(wdn, upstream, 0, 0)
    grad_before = jax.vjp(gelu_exact, before)[1](grad_hidden)[0].astype(bf16)
    part2 = dot(wup, grad_before, 1, 0)
    sg_part = jnp.sum(part2 * n2, 1)
    ss_part = jnp.sum(part2, 1)
    back2 = norm_backward(part2, n2, inv2, g2)
    back2_low = back2.astype(bf16)
    arrived = trade([cut(back2_low, (r ^ k) * tq, tq, 1) for k in range(R)], "row")
    mine = cut(back2, r * tq, tq, 1) + cut(upstream, r * tq, tq, 1).astype(f32)
    for k in range(1, R):
        blocks = arrived[k].reshape(R, db, tq)
        mine = mine + jnp.concatenate([blocks[j ^ k] for j in range(R)], 0).astype(f32)
    branch = mine.astype(bf16)
    ob_part = jnp.sum(branch.astype(f32), 1)
    grad_att = dot(wo, branch, 1, 0).astype(bf16)
    go = jnp.concatenate(
        settle(trade([cut(grad_att, (r ^ k) * W, W, 0) for k in range(R)], "row"), r), 1
    ).reshape(hp, HEAD_DIM, T)
    gox = grad_att[R * W :].reshape(X, HEAD_DIM, tq)
    branch_rows = jnp.concatenate(
        settle(trade(list(branch.reshape(R, db, tq)), "row"), r), 1
    )

    dw_down = dot(upstream, hidden, 1, 1)
    dw_up = dot(normed2, grad_before, 1, 1)
    away = jnp.stack([dw_up[:, sub:], dw_down[:, sub:]]).astype(bf16)
    home = jnp.stack([dw_up[:, :sub], dw_down[:, :sub]])
    both = (home + swap(away, "col", 1).astype(f32)).astype(bf16)
    both = both.reshape(2, R, GH, hr, sub).transpose(0, 2, 1, 3, 4).reshape(G, R, hr, sub)
    both = total(
        trade([lax.dynamic_index_in_dim(both, g ^ k, 0, False) for k in range(G)], "dp")
    ).astype(bf16)
    both = jnp.concatenate(settle(trade(list(both), "row"), r), 1)
    both = settle(spread(both, "dp"), g)
    up_weight_grad = jnp.concatenate(both[:GH], 0).astype(f32)
    down_weight_grad = jnp.concatenate(both[GH:], 0).astype(f32)

    dwo = dot(attended, branch_rows, 1, 1)
    side_rows = dwo.shape[0] // 2
    lo_o, hi_o = dwo[:side_rows], dwo[side_rows:]
    arrived = swap(jnp.where(low, hi_o, lo_o).astype(bf16), "col", 1)
    mine_o = (jnp.where(low, lo_o, hi_o) + arrived.astype(f32)).astype(bf16)
    mine_o = mine_o.reshape(G, side_rows // G, db)
    mine_o = total(
        trade([lax.dynamic_index_in_dim(mine_o, g ^ k, 0, False) for k in range(G)], "dp")
    ).astype(bf16)
    output_weight_grad = jnp.concatenate(settle(spread(mine_o, "dp"), g), 0).astype(f32)

    gq, gk, gv = attend_back(queries, keys, values, prob, go)
    gqx, gkx, gvx = attend_back(qx, kx, vx, probx, gox)
    gkv = jnp.concatenate(
        [gk.reshape(W, S), gkx.reshape(E, S), gv.reshape(W, S), gvx.reshape(E, S)], 0
    )
    gkv = (gkv[:, :T] + swap(gkv[:, T:].astype(bf16), "col", 1).astype(f32)).astype(bf16)
    gqx = lax.dynamic_update_slice_in_dim(
        jnp.zeros((E, T), bf16), gqx.reshape(E, tq).astype(bf16), r * tq, 1
    )
    grad_p = jnp.concatenate([gq.reshape(W, T).astype(bf16), gqx, gkv], 0)
    sums = jnp.sum(grad_p.astype(f32), 1)
    part1 = dot(wqkv, grad_p, 1, 0)
    fg_part = jnp.sum(part1 * n1, 1)
    fs_part = jnp.sum(part1, 1)
    back1 = norm_backward(part1, n1, inv1, g1)
    back1 = total([back1[:db]] + trade(list(back1.astype(bf16).reshape(R, db, T)), "row")[1:])
    input_grad = branch_rows.astype(f32) + back1

    dw = dot(normed1, grad_p, 1, 1)
    dq, dqx, dk, dkx, dv, dvx = jnp.split(
        dw, [W, HW, HW + W, 2 * HW, 2 * HW + W], 1
    )

    def grid(main, main_x, main_k):
        return jnp.concatenate(
            [
                pad(main[:, :half]),
                pad(main[:, half:]),
                pad(jnp.concatenate([main_x, dkx], 1)),
                pad(main_k),
            ],
            1,
        )

    lo_w, hi_w = grid(dq, dqx, dk[:, :half]), grid(dv, dvx, dk[:, half:])
    arrived = swap(jnp.where(low, hi_w, lo_w).astype(bf16), "col", 1)
    mine_w = (jnp.where(low, lo_w, hi_w) + arrived.astype(f32)).astype(bf16)
    mine_w = total(
        trade([cut(mine_w, (g ^ k) * pw, pw, 1) for k in range(G)], "dp")
    ).astype(bf16)
    mine_w = jnp.stack(settle(trade(list(mine_w.reshape(R, db, pw)), "row"), r))
    parts = settle(spread(mine_w, "dp"), g)
    ends = total([parts[2][i] for i in range(R)])
    mains = [p[:, :half].astype(f32) for i in range(R) for p in (parts[0][i], parts[1][i])]
    keys_own = jnp.stack([parts[3][i][:, :half] for i in range(R)])
    keys_other = swap(keys_own, "col", 1)
    keys_lo = jnp.where(low, keys_own, keys_other).astype(f32)
    keys_hi = jnp.where(low, keys_other, keys_own).astype(f32)
    keys_grad = jnp.concatenate(
        [p for i in range(R) for p in (keys_lo[i], keys_hi[i])] + [ends[:, E : 2 * E]], 1
    )
    main_grad = jnp.concatenate(mains + [ends[:, :E]], 1)
    qkv_weight_grad = jnp.where(
        low,
        jnp.concatenate([main_grad, keys_grad[:, :side]], 1),
        jnp.concatenate([keys_grad[:, D - side :], main_grad], 1),
    )

    rel = jnp.stack([fg_part, fs_part, ob_part, sg_part, ss_part])
    rel = jnp.concatenate(settle(jnp.split(rel, R, 1), r), 1)

    def widen(values, width, start):
        return lax.dynamic_update_slice_in_dim(jnp.zeros((width,), f32), values, start, 0)

    db_part = widen(jnp.sum(cotangent.astype(f32), 1), D, r * db)

    def placed(values):
        return jnp.concatenate([widen(values[:W], R * W, r * W), values[W:]])

    ub_sum = jnp.sum(grad_before.astype(f32), 1)
    full = up_bias.shape[0]
    ub_part = widen(ub_sum[:sub], 2 * full, c * full + r * sub) + widen(
        ub_sum[sub:], 2 * full, (1 - c) * full + r * sub
    )
    small = jnp.concatenate(
        [
            rel,
            db_part[None],
            placed(sums[:HW])[None],
            placed(sums[2 * HW :])[None],
            ub_part.reshape(-1, D),
        ],
        0,
    )
    for axis in ("col", "row", "dp"):
        k = 1
        while k < lax.axis_size(axis):
            small = small + swap(small, axis, k)
            k *= 2
    return (
        result,
        input_grad,
        small[0],
        small[1],
        qkv_weight_grad,
        small[6:8],
        output_weight_grad,
        small[2],
        small[3],
        small[4],
        up_weight_grad,
        small[8:].reshape(-1),
        down_weight_grad,
        small[5],
    )


def solution(mesh):
    placed = (
        P("row", ("dp", "col")),
        P("dp", None),
        P("row"),
        P("row"),
        P("row", "col"),
        P(),
        P("col", "row"),
        P("row"),
        P("row"),
        P("row"),
        P("row", "col"),
        P("col"),
        P("row", "col"),
        P("row"),
        P("row", ("dp", "col")),
    )
    return jax.shard_map(
        shards,
        mesh=mesh,
        in_specs=placed,
        out_specs=(
            P("row", ("dp", "col")),
            P("row", ("dp", "col")),
            P(),
            P(),
            P("row", "col"),
            P(),
            P("col", "row"),
            P(),
            P(),
            P(),
            P("row", "col"),
            P(),
            P("row", "col"),
            P(),
        ),
        check_vma=False,
    )
```

```python
import jax
import jax.numpy as jnp
from jax import lax
from jax.sharding import PartitionSpec as P

D = 1088
HEADS = 17
HEAD_DIM = 64
FF = 4352
epsilon = 1e-05
f32 = jnp.float32
bf16 = jnp.bfloat16


def gelu_exact(before):
    return jax.nn.gelu(before, approximate=False)


def dot(left, right, left_dim, right_dim):
    return lax.dot_general(
        left, right, (((left_dim,), (right_dim,)), ((), ())), preferred_element_type=f32
    )


def swap(values, axis, k):
    return lax.ppermute(values, axis, [(i, i ^ k) for i in range(lax.axis_size(axis))])


def spread(values, axis):
    return [values] + [swap(values, axis, k) for k in range(1, lax.axis_size(axis))]


def trade(pieces, axis):
    return [pieces[0]] + [swap(pieces[k], axis, k) for k in range(1, len(pieces))]


def bits(count):
    out = []
    bit = count // 2
    while bit:
        out.append(bit)
        bit //= 2
    return out


def after(values, other):
    first = lax.slice(other, (0,) * other.ndim, (1,) * other.ndim).reshape(())
    return values + (first.astype(f32) * 0.0).astype(values.dtype)


def gather_near(values, axis):
    got = {0: values}
    rows = values.shape[0]
    for bit in bits(lax.axis_size(axis)):
        names = sorted(got)
        arrived = swap(jnp.concatenate([got[k] for k in names], 0), axis, bit)
        for i, k in enumerate(names):
            got[k ^ bit] = arrived[i * rows : (i + 1) * rows]
    return [got[k] for k in range(len(got))]


def reduce_near(pieces, axis, regroup=None):
    left = dict(enumerate(pieces))
    rows = pieces[0].shape[0]
    for bit in bits(len(pieces))[::-1]:
        names = [k for k in sorted(left) if k & bit]
        sent = [left.pop(k) for k in names]
        if regroup is not None:
            sent = [regroup(piece, bit) for piece in sent]
        arrived = swap(jnp.concatenate(sent, 0).astype(bf16), axis, bit)
        for i, k in enumerate(names):
            left[k ^ bit] = left[k ^ bit] + arrived[i * rows : (i + 1) * rows].astype(f32)
    return left[0]


def gather_placed(values, axis, index, order):
    done = []
    for bit in order:
        other = swap(values, axis, bit)
        high = (index & bit) != 0
        values = jnp.stack(
            [jnp.where(high, other, values), jnp.where(high, values, other)],
            sum(1 for b in done if b > bit),
        )
        done.append(bit)
    return values.reshape((-1,) + values.shape[len(done) :])


def reduce_placed(values, axis, index, order):
    count = lax.axis_size(axis)
    names = bits(count)
    values = values.reshape((2,) * len(names) + values.shape[1:])
    for bit in order:
        place = names.index(bit)
        zero, one = [lax.index_in_dim(values, i, place, False) for i in (0, 1)]
        high = (index & bit) != 0
        arrived = swap(jnp.where(high, zero, one).astype(bf16), axis, bit)
        values = jnp.where(high, one, zero).astype(f32) + arrived.astype(f32)
        names.remove(bit)
    return values


def settle(pieces, index):
    pieces = list(pieces)
    bit = 1
    while bit < len(pieces):
        odd = (index & bit) != 0
        pieces = [jnp.where(odd, pieces[k ^ bit], pieces[k]) for k in range(len(pieces))]
        bit *= 2
    return pieces


def total(pieces):
    out = pieces[0].astype(f32)
    for piece in pieces[1:]:
        out = out + piece.astype(f32)
    return out


def cut(values, start, size, dim):
    return lax.dynamic_slice_in_dim(values, start, size, dim)


def norm_forward(rows, gain, shift):
    average = jnp.sum(rows, 0, keepdims=True) / D
    centered = rows - average
    variance = jnp.sum(centered * centered, 0, keepdims=True) / D
    inverse = lax.rsqrt(variance + epsilon)
    normal = centered * inverse
    return (normal * gain + shift).astype(bf16), normal, inverse


def norm_backward(upstream, normal, inverse, gain):
    scaled = upstream * gain
    first = jnp.sum(scaled, 0, keepdims=True) / D
    second = jnp.sum(scaled * normal, 0, keepdims=True) / D
    return inverse * (scaled - first - normal * second)


def attend(queries, keys, values, allowed):
    scores = jnp.einsum("hdk,hdq->hkq", keys, queries, preferred_element_type=f32)
    scores = jnp.where(allowed[None], scores * HEAD_DIM ** (-0.5), -1e30)
    powers = jnp.exp(scores - jnp.max(scores, 1, keepdims=True))
    probability = powers / jnp.sum(powers, 1, keepdims=True)
    out = jnp.einsum(
        "hdk,hkq->hdq", values, probability.astype(bf16), preferred_element_type=f32
    ).astype(bf16)
    return probability, out


def attend_back(queries, keys, values, probability, grad_out):
    scale = HEAD_DIM ** (-0.5)
    grad_weights = jnp.einsum("hdk,hdq->hkq", values, grad_out, preferred_element_type=f32)
    inner = jnp.sum(probability * grad_weights, 1, keepdims=True)
    grad_scores = (probability * (grad_weights - inner)).astype(bf16)
    grad_q = jnp.einsum("hdk,hkq->hdq", keys, grad_scores, preferred_element_type=f32) * scale
    grad_k = jnp.einsum("hdq,hkq->hdk", queries, grad_scores, preferred_element_type=f32) * scale
    grad_v = jnp.einsum(
        "hdq,hkq->hdk", grad_out, probability.astype(bf16), preferred_element_type=f32
    )
    return grad_q, grad_k, grad_v


def shards(
    tokens,
    block_order,
    first_gain,
    first_shift,
    qkv_weight,
    query_value_bias,
    output_weight,
    output_bias,
    second_gain,
    second_shift,
    up_weight,
    up_bias,
    down_weight,
    down_bias,
    cotangent,
):
    R, G = lax.axis_size("row"), lax.axis_size("dp")
    r, c, g = lax.axis_index("row"), lax.axis_index("col"), lax.axis_index("dp")
    low = c == 0
    db, T = tokens.shape
    tq = T // R
    hp = HEADS // R
    W = hp * HEAD_DIM
    E = HEADS * HEAD_DIM - W * R
    X = E // HEAD_DIM
    half = W // 2
    pw = max(half, 2 * E)
    sub = up_weight.shape[1] // R
    GH = G // 2
    hr = db // GH

    def pad(values):
        return jnp.pad(values, ((0, 0), (0, pw - values.shape[1])))

    x = jnp.concatenate(gather_near(tokens, "row"), 0).astype(f32)
    vectors = jnp.concatenate(
        gather_near(
            jnp.stack([first_gain, first_shift, output_bias, second_gain, second_shift]), "row"
        ),
        1,
    )
    g1, s1, ob, g2, s2 = [vectors[i][:, None] for i in range(5)]

    side = qkv_weight.shape[1] - D
    own_part = cut(qkv_weight, c * side, D, 1)
    own_keys = cut(qkv_weight, (1 - c) * D, side, 1)
    other_keys = swap(own_keys, "col", 1)
    key_part = jnp.concatenate(
        [jnp.where(low, own_keys, other_keys), jnp.where(low, other_keys, own_keys)], 1
    )
    source = jnp.where(g == 3, key_part, own_part)
    extras = pad(jnp.concatenate([own_part[:, R * W :], key_part[:, R * W :]], 1))
    offset = jnp.where(g == 3, c, g & 1) * half
    chunks = [
        jnp.where(g == 2, extras, pad(cut(source, (r ^ k) * W + offset, half, 1)))
        for k in range(R)
    ]
    piece = jnp.concatenate(trade(chunks, "row"), 0)
    own_w = jnp.concatenate(settle(spread(piece, "dp"), g), 1)
    other_w = swap(own_w, "col", 1)
    lo, hi = jnp.where(low, own_w, other_w), jnp.where(low, other_w, own_w)
    ex = 2 * pw
    kk = 3 * pw
    wqkv = jnp.concatenate(
        [
            lo[:, :half],
            lo[:, pw : pw + half],
            lo[:, ex : ex + E],
            lo[:, kk : kk + half],
            hi[:, kk : kk + half],
            lo[:, ex + E : ex + 2 * E],
            hi[:, :half],
            hi[:, pw : pw + half],
            hi[:, ex : ex + E],
        ],
        1,
    )
    HW = W + E
    bias = jnp.concatenate(
        [
            cut(query_value_bias[0], r * W, W, 0),
            query_value_bias[0, R * W :],
            jnp.zeros((HW,), f32),
            cut(query_value_bias[1], r * W, W, 0),
            query_value_bias[1, R * W :],
        ]
    )[:, None]

    part = cut(output_weight, g * (output_weight.shape[0] // G), output_weight.shape[0] // G, 0)
    part = jnp.concatenate(gather_near(after(part, x[D - db :]), "row"), 1)
    half_rows = part.shape[0] // 2
    own_o = jnp.stack(
        [
            gather_placed(part[:half_rows], "dp", g, (2, 1)),
            gather_placed(part[half_rows:], "dp", g, (1, 2)),
        ],
        1,
    ).reshape(-1, D)
    other_o = swap(own_o, "col", 1)
    wo = jnp.concatenate([jnp.where(low, own_o, other_o), jnp.where(low, other_o, own_o)], 0)

    part = jnp.where(
        g < GH,
        cut(up_weight, (g % GH) * hr, hr, 0),
        cut(down_weight, (g % GH) * hr, hr, 0),
    )
    part = after(part, x[D - db :])
    part = jnp.stack(trade([cut(part, (r ^ k) * sub, sub, 1) for k in range(R)], "row"))
    settled = part[R - 1]
    own_f = jnp.concatenate(
        [
            gather_placed(part[: R // 2], "dp", g, (2, 1)),
            gather_placed(part[R // 2 :], "dp", g, (1, 2)),
        ],
        1,
    )
    own_f = jnp.stack(
        [
            own_f[:GH].transpose(1, 0, 2, 3).reshape(D, sub),
            own_f[GH:].transpose(1, 0, 2, 3).reshape(D, sub),
        ]
    )
    wf = jnp.concatenate([own_f, swap(own_f, "col", 1)], 2)
    wup, wdn = wf[0], wf[1]
    own_ub = cut(up_bias, r * sub, sub, 0)
    ub = jnp.concatenate([own_ub, swap(own_ub, "col", 1)])[:, None]

    block = T * 2 // block_order.shape[1]
    places = (
        block_order.reshape(-1)[:, None] * block + jnp.arange(block, dtype=jnp.int32)[None, :]
    ).reshape(-1)
    own_places = cut(places, c * T, T, 0)
    key_places = jnp.concatenate([own_places, cut(places, (1 - c) * T, T, 0)])
    allowed = key_places[:, None] <= own_places[None, :]
    extra_allowed = cut(allowed, r * tq, tq, 1)

    normed1, n1, inv1 = norm_forward(x, g1, s1)
    projected = (dot(wqkv, normed1, 0, 0) + bias).astype(bf16)
    own_kv = projected[HW:]
    kv = jnp.concatenate([own_kv, swap(own_kv, "col", 1)], 1)
    S = 2 * T
    queries = projected[:W].reshape(hp, HEAD_DIM, T)
    keys = kv[:W].reshape(hp, HEAD_DIM, S)
    values = kv[HW : HW + W].reshape(hp, HEAD_DIM, S)
    qx = cut(projected[W:HW], r * tq, tq, 1).reshape(X, HEAD_DIM, tq)
    kx = kv[W:HW].reshape(X, HEAD_DIM, S)
    vx = kv[HW + W :].reshape(X, HEAD_DIM, S)
    prob, out = attend(queries, keys, values, allowed)
    probx, outx = attend(qx, kx, vx, extra_allowed)
    packed = jnp.concatenate([out.reshape(W, T), outx.reshape(E // R, T)], 0)
    rows = gather_placed(packed, "row", r, bits(R))
    attended = jnp.concatenate(
        [
            rows[:, :W].reshape(R * W, T),
            rows[:, W:].reshape(R, E, tq).transpose(1, 0, 2).reshape(E, T),
        ],
        0,
    )
    middle = x + dot(wo, attended, 0, 0) + ob
    normed2, n2, inv2 = norm_forward(middle, g2, s2)

    before = dot(wup, normed2, 0, 0) + ub
    hidden = gelu_exact(before).astype(bf16)
    down = dot(wdn, hidden, 1, 0)

    upstream = jnp.concatenate(gather_near(after(cotangent, settled), "row"), 0)
    grad_hidden = dot(wdn, upstream, 0, 0)
    grad_before = jax.vjp(gelu_exact, before)[1](grad_hidden)[0].astype(bf16)
    part2 = dot(wup, grad_before, 1, 0)
    sg_part = jnp.sum(part2 * n2, 1)
    ss_part = jnp.sum(part2, 1)
    back2 = norm_backward(part2, n2, inv2, g2)
    mine = reduce_near(
        [cut(back2, (r ^ k) * tq, tq, 1) for k in range(R)],
        "row",
        lambda piece, bit: jnp.concatenate(
            [piece[(j ^ bit) * db : ((j ^ bit) + 1) * db] for j in range(R)], 0
        ),
    )
    mine = mine + cut(upstream, r * tq, tq, 1).astype(f32)
    branch = mine.astype(bf16)
    ob_part = jnp.sum(branch.astype(f32), 1)
    grad_att = dot(wo, branch, 1, 0).astype(bf16)
    go = jnp.concatenate(
        settle(trade([cut(grad_att, (r ^ k) * W, W, 0) for k in range(R)], "row"), r), 1
    ).reshape(hp, HEAD_DIM, T)
    gox = grad_att[R * W :].reshape(X, HEAD_DIM, tq)
    branch_rows = jnp.concatenate(
        settle(trade(list(after(branch, go).reshape(R, db, tq)), "row"), r), 1
    )

    down = after(down, go)
    down = reduce_near([down[k * db : (k + 1) * db] for k in range(R)], "row")
    result = (middle[:db] + down + down_bias[:, None]).astype(bf16)

    dw_down = dot(upstream, hidden, 1, 1)
    dw_up = dot(normed2, grad_before, 1, 1)
    away = jnp.stack([dw_up[:, sub:], dw_down[:, sub:]]).astype(bf16)
    home = jnp.stack([dw_up[:, :sub], dw_down[:, :sub]])
    both = (home + swap(away, "col", 1).astype(f32)).astype(bf16)
    both = both.reshape(2, R, GH, hr, sub).transpose(0, 2, 1, 3, 4).reshape(G, R, hr, sub)
    both = jnp.concatenate(
        [
            reduce_placed(both[:, : R // 2], "dp", g, (1, 2)),
            reduce_placed(both[:, R // 2 :], "dp", g, (2, 1)),
        ],
        0,
    ).astype(bf16)
    both = settle(trade(list(both), "row"), r)
    both = jnp.concatenate(
        [
            gather_placed(jnp.concatenate(both[: R // 2], 1), "dp", g, (2, 1)),
            gather_placed(jnp.concatenate(both[R // 2 :], 1), "dp", g, (1, 2)),
        ],
        2,
    )
    up_weight_grad = both[:GH].reshape(db, -1).astype(f32)
    down_weight_grad = both[GH:].reshape(db, -1).astype(f32)

    dwo = dot(attended, branch_rows, 1, 1)
    side_rows = dwo.shape[0] // 2
    lo_o, hi_o = dwo[:side_rows], dwo[side_rows:]
    arrived = swap(jnp.where(low, hi_o, lo_o).astype(bf16), "col", 1)
    mine_o = (jnp.where(low, lo_o, hi_o) + arrived.astype(f32)).astype(bf16)
    mine_o = mine_o.reshape(G, side_rows // G, db)
    mine_o = reduce_placed(mine_o, "dp", g, (1, 2)).astype(bf16)
    output_weight_grad = (
        gather_placed(mine_o, "dp", g, (2, 1)).reshape(side_rows, db).astype(f32)
    )

    gq, gk, gv = attend_back(queries, keys, values, prob, go)
    gqx, gkx, gvx = attend_back(qx, kx, vx, probx, gox)
    gkv = jnp.concatenate(
        [gk.reshape(W, S), gkx.reshape(E, S), gv.reshape(W, S), gvx.reshape(E, S)], 0
    )
    gkv = (gkv[:, :T] + swap(gkv[:, T:].astype(bf16), "col", 1).astype(f32)).astype(bf16)
    gqx = lax.dynamic_update_slice_in_dim(
        jnp.zeros((E, T), bf16), gqx.reshape(E, tq).astype(bf16), r * tq, 1
    )
    grad_p = jnp.concatenate([gq.reshape(W, T).astype(bf16), gqx, gkv], 0)
    sums = jnp.sum(grad_p.astype(f32), 1)
    part1 = dot(wqkv, grad_p, 1, 0)
    fg_part = jnp.sum(part1 * n1, 1)
    fs_part = jnp.sum(part1, 1)
    back1 = norm_backward(part1, n1, inv1, g1)
    back1 = reduce_near([back1[k * db : (k + 1) * db] for k in range(R)], "row")
    input_grad = branch_rows.astype(f32) + back1

    dw = dot(normed1, grad_p, 1, 1)
    dq, dqx, dk, dkx, dv, dvx = jnp.split(
        dw, [W, HW, HW + W, 2 * HW, 2 * HW + W], 1
    )

    def grid(main, main_x, main_k):
        return jnp.concatenate(
            [
                pad(main[:, :half]),
                pad(main[:, half:]),
                pad(jnp.concatenate([main_x, dkx], 1)),
                pad(main_k),
            ],
            1,
        )

    lo_w, hi_w = grid(dq, dqx, dk[:, :half]), grid(dv, dvx, dk[:, half:])
    arrived = swap(jnp.where(low, hi_w, lo_w).astype(bf16), "col", 1)
    mine_w = (jnp.where(low, lo_w, hi_w) + arrived.astype(f32)).astype(bf16)
    mine_w = total(
        trade([cut(mine_w, (g ^ k) * pw, pw, 1) for k in range(G)], "dp")
    ).astype(bf16)
    mine_w = jnp.stack(settle(trade(list(mine_w.reshape(R, db, pw)), "row"), r))
    parts = settle(spread(mine_w, "dp"), g)
    ends = total([parts[2][i] for i in range(R)])
    mains = [p[:, :half].astype(f32) for i in range(R) for p in (parts[0][i], parts[1][i])]
    keys_own = jnp.stack([parts[3][i][:, :half] for i in range(R)])
    keys_other = swap(keys_own, "col", 1)
    keys_lo = jnp.where(low, keys_own, keys_other).astype(f32)
    keys_hi = jnp.where(low, keys_other, keys_own).astype(f32)
    keys_grad = jnp.concatenate(
        [p for i in range(R) for p in (keys_lo[i], keys_hi[i])] + [ends[:, E : 2 * E]], 1
    )
    main_grad = jnp.concatenate(mains + [ends[:, :E]], 1)
    qkv_weight_grad = jnp.where(
        low,
        jnp.concatenate([main_grad, keys_grad[:, :side]], 1),
        jnp.concatenate([keys_grad[:, D - side :], main_grad], 1),
    )

    rel = jnp.stack([fg_part, fs_part, ob_part, sg_part, ss_part])
    rel = jnp.concatenate(settle(jnp.split(rel, R, 1), r), 1)

    def widen(values, width, start):
        return lax.dynamic_update_slice_in_dim(jnp.zeros((width,), f32), values, start, 0)

    db_part = widen(jnp.sum(cotangent.astype(f32), 1), D, r * db)

    def placed(values):
        return jnp.concatenate([widen(values[:W], R * W, r * W), values[W:]])

    ub_sum = jnp.sum(grad_before.astype(f32), 1)
    full = up_bias.shape[0]
    ub_part = widen(ub_sum[:sub], 2 * full, c * full + r * sub) + widen(
        ub_sum[sub:], 2 * full, (1 - c) * full + r * sub
    )
    small = jnp.concatenate(
        [
            rel,
            db_part[None],
            placed(sums[:HW])[None],
            placed(sums[2 * HW :])[None],
            ub_part.reshape(-1, D),
        ],
        0,
    )
    for axis in ("col", "row", "dp"):
        k = 1
        while k < lax.axis_size(axis):
            small = small + swap(small, axis, k)
            k *= 2
    return (
        result,
        input_grad,
        small[0],
        small[1],
        qkv_weight_grad,
        small[6:8],
        output_weight_grad,
        small[2],
        small[3],
        small[4],
        up_weight_grad,
        small[8:].reshape(-1),
        down_weight_grad,
        small[5],
    )


def solution(mesh):
    placed = (
        P("row", ("dp", "col")),
        P("dp", None),
        P("row"),
        P("row"),
        P("row", "col"),
        P(),
        P("col", "row"),
        P("row"),
        P("row"),
        P("row"),
        P("row", "col"),
        P("col"),
        P("row", "col"),
        P("row"),
        P("row", ("dp", "col")),
    )
    return jax.shard_map(
        shards,
        mesh=mesh,
        in_specs=placed,
        out_specs=(
            P("row", ("dp", "col")),
            P("row", ("dp", "col")),
            P(),
            P(),
            P("row", "col"),
            P(),
            P("col", "row"),
            P(),
            P(),
            P(),
            P("row", "col"),
            P(),
            P("row", "col"),
            P(),
        ),
        check_vma=False,
    )
```

```python
import jax
import jax.numpy as jnp
from jax import lax
from jax.experimental import pallas as pl
from jax.experimental.pallas import tpu as pltpu
from jax.sharding import PartitionSpec as P

D = 1088
HEADS = 17
HEAD_DIM = 64
FF = 4352
epsilon = 1e-05
f32 = jnp.float32
bf16 = jnp.bfloat16


def gelu_exact(before):
    return jax.nn.gelu(before, approximate=False)


def dot(left, right, left_dim, right_dim):
    return lax.dot_general(
        left, right, (((left_dim,), (right_dim,)), ((), ())), preferred_element_type=f32
    )


def swap(values, axis, k):
    return lax.ppermute(values, axis, [(i, i ^ k) for i in range(lax.axis_size(axis))])


def spread(values, axis):
    return [values] + [swap(values, axis, k) for k in range(1, lax.axis_size(axis))]


def trade(pieces, axis):
    return [pieces[0]] + [swap(pieces[k], axis, k) for k in range(1, len(pieces))]


def bits(count):
    out = []
    bit = count // 2
    while bit:
        out.append(bit)
        bit //= 2
    return out


def after(values, other):
    first = lax.slice(other, (0,) * other.ndim, (1,) * other.ndim).reshape(())
    return values + (first.astype(f32) * 0.0).astype(values.dtype)


def gather_near(values, axis, hold=None):
    got = {0: values}
    rows = values.shape[0]
    for bit in bits(lax.axis_size(axis)):
        names = sorted(got)
        sent = jnp.concatenate([got[k] for k in names], 0)
        if hold is not None and len(names) > 1:
            sent = hold(sent)
        arrived = swap(sent, axis, bit)
        for i, k in enumerate(names):
            got[k ^ bit] = arrived[i * rows : (i + 1) * rows]
    return [got[k] for k in range(len(got))]


def reduce_near(pieces, axis, regroup=None):
    left = dict(enumerate(pieces))
    rows = pieces[0].shape[0]
    for bit in bits(len(pieces))[::-1]:
        names = [k for k in sorted(left) if k & bit]
        sent = [left.pop(k) for k in names]
        if regroup is not None:
            sent = [regroup(piece, bit) for piece in sent]
        arrived = swap(jnp.concatenate(sent, 0).astype(bf16), axis, bit)
        for i, k in enumerate(names):
            left[k ^ bit] = left[k ^ bit] + arrived[i * rows : (i + 1) * rows].astype(f32)
    return left[0]


def gather_placed(values, axis, index, order):
    done = []
    for bit in order:
        other = swap(values, axis, bit)
        high = (index & bit) != 0
        values = jnp.stack(
            [jnp.where(high, other, values), jnp.where(high, values, other)],
            sum(1 for b in done if b > bit),
        )
        done.append(bit)
    return values.reshape((-1,) + values.shape[len(done) :])


def reduce_placed(values, axis, index, order, steps=False):
    count = lax.axis_size(axis)
    names = bits(count)
    values = values.reshape((2,) * len(names) + values.shape[1:])
    for bit in order:
        place = names.index(bit)
        zero, one = [lax.index_in_dim(values, i, place, False) for i in (0, 1)]
        high = (index & bit) != 0
        arrived = swap(jnp.where(high, zero, one).astype(bf16), axis, bit)
        values = jnp.where(high, one, zero).astype(f32) + arrived.astype(f32)
        names.remove(bit)
        if steps and bit == order[0]:
            stage = arrived
    return (values, stage) if steps else values


def settle(pieces, index):
    pieces = list(pieces)
    bit = 1
    while bit < len(pieces):
        odd = (index & bit) != 0
        pieces = [jnp.where(odd, pieces[k ^ bit], pieces[k]) for k in range(len(pieces))]
        bit *= 2
    return pieces


def total(pieces):
    out = pieces[0].astype(f32)
    for piece in pieces[1:]:
        out = out + piece.astype(f32)
    return out


def cut(values, start, size, dim):
    return lax.dynamic_slice_in_dim(values, start, size, dim)


def norm_forward(rows, gain, shift):
    average = jnp.sum(rows, 0, keepdims=True) / D
    centered = rows - average
    variance = jnp.sum(centered * centered, 0, keepdims=True) / D
    inverse = lax.rsqrt(variance + epsilon)
    normal = centered * inverse
    return (normal * gain + shift).astype(bf16), normal, inverse


def norm_backward(upstream, normal, inverse, gain):
    scaled = upstream * gain
    first = jnp.sum(scaled, 0, keepdims=True) / D
    second = jnp.sum(scaled * normal, 0, keepdims=True) / D
    return inverse * (scaled - first - normal * second)


SCALE = HEAD_DIM ** (-0.5)


def masked(keys, scaled, key_rank, query_rank):
    scores = dot(keys, scaled, 0, 0)
    return jnp.where(key_rank <= query_rank, scores, -1e30)


def attend_kernel(q, k0, v0, k1, v1, query_rank, rank0, rank1, out, log_total):
    scaled = q[...] * jnp.asarray(SCALE, bf16)
    query = query_rank[...]
    s0 = masked(k0[...], scaled, rank0[...], query)
    s1 = masked(k1[...], scaled, rank1[...], query)
    largest = jnp.maximum(jnp.max(s0, 0, keepdims=True), jnp.max(s1, 0, keepdims=True))
    p0 = jnp.exp(s0 - largest)
    p1 = jnp.exp(s1 - largest)
    totals = jnp.sum(p0, 0, keepdims=True) + jnp.sum(p1, 0, keepdims=True)
    got = dot(v0[...], p0.astype(bf16), 1, 0) + dot(v1[...], p1.astype(bf16), 1, 0)
    out[...] = (got / totals).astype(bf16)
    log_total[...] = (largest + jnp.log(totals))[None]


def back_kernel(
    q, k0, v0, k1, v1, query_rank, rank0, rank1, log_total, grad, gq, gk0, gv0, gk1, gv1, sums
):
    step = pl.program_id(1)

    @pl.when(step == 0)
    def _():
        sums[...] = jnp.zeros_like(sums)

    scaled = q[...] * jnp.asarray(SCALE, bf16)
    query = query_rank[...]
    shift = log_total[...][0]
    g = grad[...]
    p0 = jnp.exp(masked(k0[...], scaled, rank0[...], query) - shift)
    p1 = jnp.exp(masked(k1[...], scaled, rank1[...], query) - shift)
    w0 = dot(v0[...], g, 0, 0)
    w1 = dot(v1[...], g, 0, 0)
    inner = jnp.sum(p0 * w0, 0, keepdims=True) + jnp.sum(p1 * w1, 0, keepdims=True)
    d0 = (p0 * (w0 - inner)).astype(bf16)
    d1 = (p1 * (w1 - inner)).astype(bf16)
    gq[...] = ((dot(k0[...], d0, 1, 0) + dot(k1[...], d1, 1, 0)) * SCALE).astype(gq.dtype)
    sums[0] += dot(scaled, d0, 1, 1)
    sums[1] += dot(g, p0.astype(bf16), 1, 1)
    sums[2] += dot(scaled, d1, 1, 1)
    sums[3] += dot(g, p1.astype(bf16), 1, 1)

    @pl.when(step == pl.num_programs(1) - 1)
    def _():
        gk0[...] = sums[0].astype(gk0.dtype)
        gv0[...] = sums[1].astype(gv0.dtype)
        gk1[...] = sums[2].astype(gk1.dtype)
        gv1[...] = sums[3].astype(gv1.dtype)


def attention_specs(width, T, first, all_heads):
    def key_spec(at):
        return pl.BlockSpec((HEAD_DIM, T), lambda h, i: (at + h, 0))

    row = pl.BlockSpec((HEAD_DIM, width), lambda h, i: (h, i))
    ranks = [pl.BlockSpec((1, width), lambda h, i: (0, i))] + [
        pl.BlockSpec((T, 1), lambda h, i: (0, 0))
    ] * 2
    pair = [key_spec(first), key_spec(all_heads + first)]
    return row, [row] + pair + pair + ranks


def attend(queries, kv0, kv1, query_rank, rank0, rank1, first):
    heads, t = queries.shape[0] // HEAD_DIM, queries.shape[1]
    T = kv0.shape[1]
    width = min(t, 512)
    row, specs = attention_specs(width, T, first, kv0.shape[0] // HEAD_DIM // 2)
    size = heads * t * 2 * T
    return pl.pallas_call(
        attend_kernel,
        grid=(heads, t // width),
        in_specs=specs,
        out_specs=[row, pl.BlockSpec((1, 1, width), lambda h, i: (h, 0, i))],
        out_shape=[
            jax.ShapeDtypeStruct(queries.shape, bf16),
            jax.ShapeDtypeStruct((heads, 1, t), f32),
        ],
        compiler_params=pltpu.CompilerParams(vmem_limit_bytes=40 * 2**20),
        cost_estimate=pl.CostEstimate(
            flops=size * 4 * HEAD_DIM * 4, bytes_accessed=4 * kv0.size, transcendentals=size
        ),
    )(queries, kv0, kv0, kv1, kv1, query_rank, rank0, rank1)


def attend_back(queries, kv0, kv1, query_rank, rank0, rank1, first, log_total, grad):
    heads, t = queries.shape[0] // HEAD_DIM, queries.shape[1]
    T = kv0.shape[1]
    width = min(t, 512)
    row, specs = attention_specs(width, T, first, kv0.shape[0] // HEAD_DIM // 2)
    size = heads * t * 2 * T
    grads = pl.BlockSpec((HEAD_DIM, T), lambda h, i: (h, 0))
    return pl.pallas_call(
        back_kernel,
        grid=(heads, t // width),
        in_specs=specs + [pl.BlockSpec((1, 1, width), lambda h, i: (h, 0, i)), row],
        out_specs=[row] + [grads] * 4,
        out_shape=[jax.ShapeDtypeStruct(queries.shape, bf16)]
        + [jax.ShapeDtypeStruct((heads * HEAD_DIM, T), d) for d in (f32, f32, bf16, bf16)],
        scratch_shapes=[pltpu.VMEM((4, HEAD_DIM, T), f32)],
        compiler_params=pltpu.CompilerParams(vmem_limit_bytes=48 * 2**20),
        cost_estimate=pl.CostEstimate(
            flops=size * 10 * HEAD_DIM * 4, bytes_accessed=8 * kv0.size, transcendentals=size
        ),
    )(queries, kv0, kv0, kv1, kv1, query_rank, rank0, rank1, log_total, grad)


def shards(
    tokens,
    block_order,
    first_gain,
    first_shift,
    qkv_weight,
    query_value_bias,
    output_weight,
    output_bias,
    second_gain,
    second_shift,
    up_weight,
    up_bias,
    down_weight,
    down_bias,
    cotangent,
):
    R, G = lax.axis_size("row"), lax.axis_size("dp")
    r, c, g = lax.axis_index("row"), lax.axis_index("col"), lax.axis_index("dp")
    low = c == 0
    db, T = tokens.shape
    tq = T // R
    hp = HEADS // R
    W = hp * HEAD_DIM
    E = HEADS * HEAD_DIM - W * R
    X = E // HEAD_DIM
    half = W // 2
    pw = max(half, 2 * E)
    sub = up_weight.shape[1] // R
    GH = G // 2
    hr = db // GH

    def pad(values):
        return jnp.pad(values, ((0, 0), (0, pw - values.shape[1])))

    x = jnp.concatenate(gather_near(tokens, "row"), 0).astype(f32)
    vectors = jnp.concatenate(
        gather_near(
            jnp.stack([first_gain, first_shift, output_bias, second_gain, second_shift]), "row"
        ),
        1,
    )
    g1, s1, ob, g2, s2 = [vectors[i][:, None] for i in range(5)]

    side = qkv_weight.shape[1] - D
    own_part = cut(qkv_weight, c * side, D, 1)
    own_keys = cut(qkv_weight, (1 - c) * D, side, 1)
    other_keys = swap(own_keys, "col", 1)
    key_part = jnp.concatenate(
        [jnp.where(low, own_keys, other_keys), jnp.where(low, other_keys, own_keys)], 1
    )
    source = jnp.where(g == 3, key_part, own_part)
    extra_keys = jnp.where(low, key_part[:, R * W :], 0)
    extras = pad(jnp.concatenate([own_part[:, R * W :], extra_keys], 1))
    offset = jnp.where(g == 3, c, g & 1) * half
    chunks = [
        jnp.where(g == 2, extras, pad(cut(source, (r ^ k) * W + offset, half, 1)))
        for k in range(R)
    ]
    piece = jnp.concatenate(trade(chunks, "row"), 0)
    own_w = jnp.concatenate(settle(spread(piece, "dp"), g), 1)
    other_w = swap(own_w, "col", 1)
    lo, hi = jnp.where(low, own_w, other_w), jnp.where(low, other_w, own_w)
    wqkv = jnp.concatenate([lo, hi], 1)
    HW = W + E
    ex = 2 * pw
    kk = 3 * pw
    end = 4 * pw

    def arrange(main, main_x, extra_k, main_k):
        def fill(values):
            return jnp.pad(values, ((0, pw - values.shape[0]), (0, 0)))

        return [
            fill(main[:half]),
            fill(main[half:]),
            fill(jnp.concatenate([main_x, extra_k], 0)),
            fill(main_k),
        ]

    def bias_rows(values):
        nothing = jnp.zeros((E, 1), f32)
        return arrange(cut(values, r * W, W, 0), values[R * W :], nothing, nothing)

    bias = jnp.concatenate(
        [p for i in (0, 1) for p in bias_rows(query_value_bias[i][:, None])], 0
    )

    block = T * 2 // block_order.shape[1]
    places = (
        block_order.reshape(-1)[:, None] * block + jnp.arange(block, dtype=jnp.int32)[None, :]
    ).reshape(-1)
    own_places = cut(places, c * T, T, 0)
    other_places = cut(places, (1 - c) * T, T, 0)
    rank0, rank1 = own_places[:, None], other_places[:, None]
    query_rank = own_places[None, :]
    extra_rank = cut(query_rank, r * tq, tq, 1)

    normed1, n1, inv1 = norm_forward(x, g1, s1)
    projected = (dot(wqkv, normed1, 0, 0) + bias).astype(bf16)

    def rows_of(at, size):
        return projected[at : at + size]

    queries = jnp.concatenate([rows_of(0, half), rows_of(pw, half)], 0)
    queries_x = cut(rows_of(ex, E), r * tq, tq, 1)
    kv0 = jnp.concatenate(
        [
            rows_of(kk, half),
            rows_of(end + kk, half),
            rows_of(ex + E, E),
            rows_of(end, half),
            rows_of(end + pw, half),
            rows_of(end + ex, E),
        ],
        0,
    )
    kv1 = swap(kv0, "col", 1)
    outx, log_x = attend(queries_x, kv0, kv1, extra_rank, rank0, rank1, hp)
    out, log_main = attend(queries, kv0, kv1, query_rank, rank0, rank1, 0)
    part = cut(output_weight, g * (output_weight.shape[0] // G), output_weight.shape[0] // G, 0)
    part = jnp.concatenate(
        gather_near(after(part, x[D - db :]), "row", lambda v: after(v, projected)), 1
    )
    part = after(part, kv1)
    half_rows = part.shape[0] // 2
    own_o = jnp.stack(
        [
            gather_placed(part[:half_rows], "dp", g, (2, 1)),
            gather_placed(part[half_rows:], "dp", g, (1, 2)),
        ],
        1,
    ).reshape(-1, D)
    other_o = swap(own_o, "col", 1)
    wo = jnp.concatenate([jnp.where(low, own_o, other_o), jnp.where(low, other_o, own_o)], 0)

    part = jnp.where(
        g < GH,
        cut(up_weight, (g % GH) * hr, hr, 0),
        cut(down_weight, (g % GH) * hr, hr, 0),
    )
    part = after(part, x[D - db :])
    part = jnp.stack(trade([cut(part, (r ^ k) * sub, sub, 1) for k in range(R)], "row"))
    part = after(part, projected)
    own_f = jnp.concatenate(
        [
            gather_placed(part[: R // 2], "dp", g, (2, 1)),
            gather_placed(part[R // 2 :], "dp", g, (1, 2)),
        ],
        1,
    )
    own_f = jnp.stack(
        [
            own_f[:GH].transpose(1, 0, 2, 3).reshape(D, sub),
            own_f[GH:].transpose(1, 0, 2, 3).reshape(D, sub),
        ]
    )
    own_f = after(own_f, outx)
    wf = jnp.concatenate([own_f, swap(own_f, "col", 1)], 2)
    wup, wdn = wf[0], wf[1]
    own_ub = cut(up_bias, r * sub, sub, 0)
    ub = jnp.concatenate([own_ub, swap(own_ub, "col", 1)])[:, None]

    packed = jnp.concatenate([out, outx.reshape(E // R, T)], 0)
    rows = gather_placed(packed, "row", r, bits(R))
    attended = jnp.concatenate(
        [
            rows[:, :W].reshape(R * W, T),
            rows[:, W:].reshape(R, E, tq).transpose(1, 0, 2).reshape(E, T),
        ],
        0,
    )
    middle = x + dot(wo, attended, 0, 0) + ob
    normed2, n2, inv2 = norm_forward(middle, g2, s2)

    before = dot(wup, normed2, 0, 0) + ub
    hidden = gelu_exact(before).astype(bf16)
    down = dot(wdn, hidden, 1, 0)

    upstream = jnp.concatenate(gather_near(after(cotangent, projected), "row"), 0)
    grad_hidden = dot(wdn, upstream, 0, 0)
    grad_before = jax.vjp(gelu_exact, before)[1](grad_hidden)[0].astype(bf16)
    part2 = dot(wup, grad_before, 1, 0)
    sg_part = jnp.sum(part2 * n2, 1)
    ss_part = jnp.sum(part2, 1)
    back2 = norm_backward(part2, n2, inv2, g2)
    mine = reduce_near(
        [cut(back2, (r ^ k) * tq, tq, 1) for k in range(R)],
        "row",
        lambda piece, bit: jnp.concatenate(
            [piece[(j ^ bit) * db : ((j ^ bit) + 1) * db] for j in range(R)], 0
        ),
    )
    mine = mine + cut(upstream, r * tq, tq, 1).astype(f32)
    branch = mine.astype(bf16)
    ob_part = jnp.sum(branch.astype(f32), 1)
    grad_att = dot(wo, branch, 1, 0).astype(bf16)
    go = jnp.concatenate(
        settle(trade([cut(grad_att, (r ^ k) * W, W, 0) for k in range(R)], "row"), r), 1
    )
    gox = grad_att[R * W :]
    branch_rows = jnp.concatenate(
        settle(trade(list(after(branch, go).reshape(R, db, tq)), "row"), r), 1
    )

    down = after(down, mine)
    down = reduce_near([down[k * db : (k + 1) * db] for k in range(R)], "row")
    result = (middle[:db] + down + down_bias[:, None]).astype(bf16)

    dw_down = dot(upstream, hidden, 1, 1)
    dw_up = dot(normed2, grad_before, 1, 1)
    away = jnp.stack([dw_up[:, sub:], dw_down[:, sub:]]).astype(bf16)
    home = jnp.stack([dw_up[:, :sub], dw_down[:, :sub]])
    both = (home + swap(away, "col", 1).astype(f32)).astype(bf16)
    both = both.reshape(2, R, GH, hr, sub).transpose(0, 2, 1, 3, 4).reshape(G, R, hr, sub)
    first, stage = reduce_placed(both[:, : R // 2], "dp", g, (1, 2), True)
    second, _ = reduce_placed(both[:, R // 2 :], "dp", g, (2, 1), True)
    both = jnp.concatenate([first, second], 0).astype(bf16)
    late = both
    both = settle(trade(list(both), "row"), r)
    both = jnp.concatenate(
        [
            gather_placed(jnp.concatenate(both[: R // 2], 1), "dp", g, (2, 1)),
            gather_placed(jnp.concatenate(both[R // 2 :], 1), "dp", g, (1, 2)),
        ],
        2,
    )
    up_weight_grad = both[:GH].reshape(db, -1).astype(f32)
    down_weight_grad = both[GH:].reshape(db, -1).astype(f32)

    dwo = dot(attended, branch_rows, 1, 1)
    side_rows = dwo.shape[0] // 2
    lo_o, hi_o = dwo[:side_rows], dwo[side_rows:]
    arrived = swap(jnp.where(low, hi_o, lo_o).astype(bf16), "col", 1)
    mine_o = (jnp.where(low, lo_o, hi_o) + arrived.astype(f32)).astype(bf16)
    mine_o = mine_o.reshape(G, side_rows // G, db)
    mine_o = reduce_placed(mine_o, "dp", g, (1, 2)).astype(bf16)
    output_weight_grad = (
        gather_placed(mine_o, "dp", g, (2, 1)).reshape(side_rows, db).astype(f32)
    )

    log_main = after(log_main, stage)
    gqx, *gx = attend_back(
        queries_x, kv0, kv1, extra_rank, rank0, rank1, hp, log_x, gox
    )
    gq, *gm = attend_back(queries, kv0, kv1, query_rank, rank0, rank1, 0, log_main, go)
    away = jnp.concatenate([gm[2], gx[2], gm[3], gx[3]], 0)
    arrived = swap(after(away, late), "col", 1)
    gkv = (jnp.concatenate([gm[0], gx[0], gm[1], gx[1]], 0) + arrived.astype(f32)).astype(bf16)
    gqx = lax.dynamic_update_slice_in_dim(jnp.zeros((E, T), bf16), gqx, r * tq, 1)
    gk, gkx, gv, gvx = gkv[:W], gkv[W:HW], gkv[HW : HW + W], gkv[HW + W :]
    grad_p = jnp.concatenate(
        arrange(gq, gqx, gkx, gk[:half]) + arrange(gv, gvx, gkx, gk[half:]), 0
    )
    sums = jnp.sum(grad_p.astype(f32), 1)
    part1 = dot(wqkv, grad_p, 1, 0)
    fg_part = jnp.sum(part1 * n1, 1)
    fs_part = jnp.sum(part1, 1)
    back1 = norm_backward(part1, n1, inv1, g1)
    back1 = reduce_near([back1[k * db : (k + 1) * db] for k in range(R)], "row")
    input_grad = branch_rows.astype(f32) + back1

    dw = dot(normed1, grad_p, 1, 1)
    lo_w, hi_w = dw[:, :end], dw[:, end:]
    arrived = swap(jnp.where(low, hi_w, lo_w).astype(bf16), "col", 1)
    mine_w = (jnp.where(low, lo_w, hi_w) + arrived.astype(f32)).astype(bf16)
    mine_w = total(
        trade([cut(mine_w, (g ^ k) * pw, pw, 1) for k in range(G)], "dp")
    ).astype(bf16)
    mine_w = jnp.stack(settle(trade(list(mine_w.reshape(R, db, pw)), "row"), r))
    parts = settle(spread(mine_w, "dp"), g)
    ends = total([parts[2][i] for i in range(R)])
    mains = [p[:, :half].astype(f32) for i in range(R) for p in (parts[0][i], parts[1][i])]
    keys_own = jnp.stack([parts[3][i][:, :half] for i in range(R)])
    keys_other = swap(keys_own, "col", 1)
    keys_lo = jnp.where(low, keys_own, keys_other).astype(f32)
    keys_hi = jnp.where(low, keys_other, keys_own).astype(f32)
    keys_grad = jnp.concatenate(
        [p for i in range(R) for p in (keys_lo[i], keys_hi[i])] + [ends[:, E : 2 * E]], 1
    )
    main_grad = jnp.concatenate(mains + [ends[:, :E]], 1)
    qkv_weight_grad = jnp.where(
        low,
        jnp.concatenate([main_grad, keys_grad[:, :side]], 1),
        jnp.concatenate([keys_grad[:, D - side :], main_grad], 1),
    )

    rel = jnp.stack([fg_part, fs_part, ob_part, sg_part, ss_part])
    rel = jnp.concatenate(settle(jnp.split(rel, R, 1), r), 1)

    def widen(values, width, start):
        return lax.dynamic_update_slice_in_dim(jnp.zeros((width,), f32), values, start, 0)

    db_part = widen(jnp.sum(cotangent.astype(f32), 1), D, r * db)

    def placed(at):
        main = jnp.concatenate([sums[at : at + half], sums[at + pw : at + pw + half]])
        return jnp.concatenate([widen(main, R * W, r * W), sums[at + ex : at + ex + E]])

    ub_sum = jnp.sum(grad_before.astype(f32), 1)
    full = up_bias.shape[0]
    ub_part = widen(ub_sum[:sub], 2 * full, c * full + r * sub) + widen(
        ub_sum[sub:], 2 * full, (1 - c) * full + r * sub
    )
    small = jnp.concatenate(
        [
            rel,
            db_part[None],
            placed(0)[None],
            placed(end)[None],
            ub_part.reshape(-1, D),
        ],
        0,
    )
    for axis in ("col", "row", "dp"):
        k = 1
        while k < lax.axis_size(axis):
            small = small + swap(small, axis, k)
            k *= 2
    return (
        result,
        input_grad,
        small[0],
        small[1],
        qkv_weight_grad,
        small[6:8],
        output_weight_grad,
        small[2],
        small[3],
        small[4],
        up_weight_grad,
        small[8:].reshape(-1),
        down_weight_grad,
        small[5],
    )


def solution(mesh):
    placed = (
        P("row", ("dp", "col")),
        P("dp", None),
        P("row"),
        P("row"),
        P("row", "col"),
        P(),
        P("col", "row"),
        P("row"),
        P("row"),
        P("row"),
        P("row", "col"),
        P("col"),
        P("row", "col"),
        P("row"),
        P("row", ("dp", "col")),
    )
    return jax.shard_map(
        shards,
        mesh=mesh,
        in_specs=placed,
        out_specs=(
            P("row", ("dp", "col")),
            P("row", ("dp", "col")),
            P(),
            P(),
            P("row", "col"),
            P(),
            P("col", "row"),
            P(),
            P(),
            P(),
            P("row", "col"),
            P(),
            P("row", "col"),
            P(),
        ),
        check_vma=False,
    )
```

```python
import jax
import jax.numpy as jnp
from jax import lax
from jax.experimental import pallas as pl
from jax.experimental.layout import Layout, with_layout_constraint
from jax.experimental.pallas import tpu as pltpu
from jax.sharding import PartitionSpec as P

D = 1088
HEADS = 17
HEAD_DIM = 64
FF = 4352
epsilon = 1e-05
f32 = jnp.float32
bf16 = jnp.bfloat16


def gelu_pair(before):
    below = 0.5 + 0.5 * lax.erf(before * 0.5**0.5)
    density = jnp.exp(-0.5 * before * before) * (0.5 / jnp.pi) ** 0.5
    return (before * below).astype(bf16), below + before * density


def dot(left, right, left_dim, right_dim):
    return lax.dot_general(
        left, right, (((left_dim,), (right_dim,)), ((), ())), preferred_element_type=f32
    )


def plain(values):
    return with_layout_constraint(values, Layout(tuple(range(values.ndim))))


def swap(values, axis, k):
    pairs = [(i, i ^ k) for i in range(lax.axis_size(axis))]
    return plain(lax.ppermute(plain(values), axis, pairs))


def spread(values, axis):
    return [values] + [swap(values, axis, k) for k in range(1, lax.axis_size(axis))]


def trade(pieces, axis):
    return [pieces[0]] + [swap(pieces[k], axis, k) for k in range(1, len(pieces))]


def bits(count):
    out = []
    bit = count // 2
    while bit:
        out.append(bit)
        bit //= 2
    return out


def after(values, other):
    first = lax.slice(other, (0,) * other.ndim, (1,) * other.ndim).reshape(())
    return values + (first.astype(f32) * 0.0).astype(values.dtype)


def gather_near(values, axis, hold=None):
    got = {0: values}
    rows = values.shape[0]
    for bit in bits(lax.axis_size(axis)):
        names = sorted(got)
        sent = jnp.concatenate([got[k] for k in names], 0)
        if hold is not None and len(names) > 1:
            sent = hold(sent)
        arrived = swap(sent, axis, bit)
        for i, k in enumerate(names):
            got[k ^ bit] = arrived[i * rows : (i + 1) * rows]
    return [got[k] for k in range(len(got))]


def reduce_near(pieces, axis, regroup=None, hold=None):
    left = dict(enumerate(pieces))
    rows = pieces[0].shape[0]
    for bit in bits(len(pieces))[::-1]:
        names = [k for k in sorted(left) if k & bit]
        sent = [left.pop(k) for k in names]
        if regroup is not None:
            sent = [regroup(piece, bit) for piece in sent]
        sent = jnp.concatenate(sent, 0).astype(bf16)
        if hold is not None and len(names) == 1:
            sent = hold(sent)
        arrived = swap(sent, axis, bit)
        for i, k in enumerate(names):
            left[k ^ bit] = left[k ^ bit] + arrived[i * rows : (i + 1) * rows].astype(f32)
    return left[0]


def gather_placed(values, axis, index, order, hold=None):
    done = []
    for bit in order:
        if hold is not None and done:
            values = hold(values)
        other = swap(values, axis, bit)
        high = (index & bit) != 0
        values = jnp.stack(
            [jnp.where(high, other, values), jnp.where(high, values, other)],
            sum(1 for b in done if b > bit),
        )
        done.append(bit)
    return values.reshape((-1,) + values.shape[len(done) :])


def reduce_placed(values, axis, index, order, steps=False):
    count = lax.axis_size(axis)
    names = bits(count)
    values = values.reshape((2,) * len(names) + values.shape[1:])
    for bit in order:
        place = names.index(bit)
        zero, one = [lax.index_in_dim(values, i, place, False) for i in (0, 1)]
        high = (index & bit) != 0
        arrived = swap(jnp.where(high, zero, one).astype(bf16), axis, bit)
        values = jnp.where(high, one, zero).astype(f32) + arrived.astype(f32)
        names.remove(bit)
        if steps and bit == order[0]:
            stage = arrived
    return (values, stage) if steps else values


def settle(pieces, index):
    pieces = list(pieces)
    bit = 1
    while bit < len(pieces):
        odd = (index & bit) != 0
        pieces = [jnp.where(odd, pieces[k ^ bit], pieces[k]) for k in range(len(pieces))]
        bit *= 2
    return pieces


def total(pieces):
    out = pieces[0].astype(f32)
    for piece in pieces[1:]:
        out = out + piece.astype(f32)
    return out


def cut(values, start, size, dim):
    return lax.dynamic_slice_in_dim(values, start, size, dim)


def norm_forward(rows, gain, shift):
    average = jnp.sum(rows, 0, keepdims=True) / D
    centered = rows - average
    variance = jnp.sum(centered * centered, 0, keepdims=True) / D
    inverse = lax.rsqrt(variance + epsilon)
    normal = centered * inverse
    return (normal * gain + shift).astype(bf16), normal, inverse


def norm_backward(upstream, normal, inverse, gain):
    scaled = upstream * gain
    first = jnp.sum(scaled, 0, keepdims=True) / D
    second = jnp.sum(scaled * normal, 0, keepdims=True) / D
    return inverse * (scaled - first - normal * second)


SCALE = HEAD_DIM ** (-0.5)


def masked(keys, scaled, key_rank, query_rank):
    scores = dot(keys, scaled, 0, 0)
    return jnp.where(key_rank <= query_rank, scores, -1e30)


def attend_kernel(q, k0, v0, k1, v1, query_rank, rank0, rank1, out, log_total):
    scaled = q[...] * jnp.asarray(SCALE, bf16)
    query = query_rank[...]
    s0 = masked(k0[...], scaled, rank0[...], query)
    s1 = masked(k1[...], scaled, rank1[...], query)
    largest = jnp.maximum(jnp.max(s0, 0, keepdims=True), jnp.max(s1, 0, keepdims=True))
    p0 = jnp.exp(s0 - largest)
    p1 = jnp.exp(s1 - largest)
    totals = jnp.sum(p0, 0, keepdims=True) + jnp.sum(p1, 0, keepdims=True)
    got = dot(v0[...], p0.astype(bf16), 1, 0) + dot(v1[...], p1.astype(bf16), 1, 0)
    out[...] = (got / totals).astype(bf16)
    log_total[...] = (largest + jnp.log(totals))[None]


def back_kernel(
    q, k0, v0, k1, v1, query_rank, rank0, rank1, log_total, grad, gq, gk0, gv0, gk1, gv1, sums
):
    step = pl.program_id(1)

    @pl.when(step == 0)
    def _():
        sums[...] = jnp.zeros_like(sums)

    scaled = q[...] * jnp.asarray(SCALE, bf16)
    query = query_rank[...]
    shift = log_total[...][0]
    g = grad[...]
    p0 = jnp.exp(masked(k0[...], scaled, rank0[...], query) - shift)
    p1 = jnp.exp(masked(k1[...], scaled, rank1[...], query) - shift)
    w0 = dot(v0[...], g, 0, 0)
    w1 = dot(v1[...], g, 0, 0)
    inner = jnp.sum(p0 * w0, 0, keepdims=True) + jnp.sum(p1 * w1, 0, keepdims=True)
    d0 = (p0 * (w0 - inner)).astype(bf16)
    d1 = (p1 * (w1 - inner)).astype(bf16)
    gq[...] = ((dot(k0[...], d0, 1, 0) + dot(k1[...], d1, 1, 0)) * SCALE).astype(gq.dtype)
    sums[0] += dot(scaled, d0, 1, 1)
    sums[1] += dot(g, p0.astype(bf16), 1, 1)
    sums[2] += dot(scaled, d1, 1, 1)
    sums[3] += dot(g, p1.astype(bf16), 1, 1)

    @pl.when(step == pl.num_programs(1) - 1)
    def _():
        gk0[...] = sums[0].astype(gk0.dtype)
        gv0[...] = sums[1].astype(gv0.dtype)
        gk1[...] = sums[2].astype(gk1.dtype)
        gv1[...] = sums[3].astype(gv1.dtype)


def attention_specs(width, T, first, all_heads):
    def key_spec(at):
        return pl.BlockSpec((HEAD_DIM, T), lambda h, i: (at + h, 0))

    row = pl.BlockSpec((HEAD_DIM, width), lambda h, i: (h, i))
    ranks = [pl.BlockSpec((1, width), lambda h, i: (0, i))] + [
        pl.BlockSpec((T, 1), lambda h, i: (0, 0))
    ] * 2
    pair = [key_spec(first), key_spec(all_heads + first)]
    return row, [row] + pair + pair + ranks


def attend(queries, kv0, kv1, query_rank, rank0, rank1, first):
    heads, t = queries.shape[0] // HEAD_DIM, queries.shape[1]
    T = kv0.shape[1]
    width = min(t, 512)
    row, specs = attention_specs(width, T, first, kv0.shape[0] // HEAD_DIM // 2)
    size = heads * t * 2 * T
    return pl.pallas_call(
        attend_kernel,
        grid=(heads, t // width),
        in_specs=specs,
        out_specs=[row, pl.BlockSpec((1, 1, width), lambda h, i: (h, 0, i))],
        out_shape=[
            jax.ShapeDtypeStruct(queries.shape, bf16),
            jax.ShapeDtypeStruct((heads, 1, t), f32),
        ],
        compiler_params=pltpu.CompilerParams(vmem_limit_bytes=40 * 2**20),
        cost_estimate=pl.CostEstimate(
            flops=size * 4 * HEAD_DIM * 4, bytes_accessed=4 * kv0.size, transcendentals=size
        ),
    )(queries, kv0, kv0, kv1, kv1, query_rank, rank0, rank1)


def attend_back(queries, kv0, kv1, query_rank, rank0, rank1, first, log_total, grad):
    heads, t = queries.shape[0] // HEAD_DIM, queries.shape[1]
    T = kv0.shape[1]
    width = min(t, 512)
    row, specs = attention_specs(width, T, first, kv0.shape[0] // HEAD_DIM // 2)
    size = heads * t * 2 * T
    grads = pl.BlockSpec((HEAD_DIM, T), lambda h, i: (h, 0))
    return pl.pallas_call(
        back_kernel,
        grid=(heads, t // width),
        in_specs=specs + [pl.BlockSpec((1, 1, width), lambda h, i: (h, 0, i)), row],
        out_specs=[row] + [grads] * 4,
        out_shape=[jax.ShapeDtypeStruct(queries.shape, bf16)]
        + [jax.ShapeDtypeStruct((heads * HEAD_DIM, T), d) for d in (f32, f32, bf16, bf16)],
        scratch_shapes=[pltpu.VMEM((4, HEAD_DIM, T), f32)],
        compiler_params=pltpu.CompilerParams(vmem_limit_bytes=48 * 2**20),
        cost_estimate=pl.CostEstimate(
            flops=size * 10 * HEAD_DIM * 4, bytes_accessed=8 * kv0.size, transcendentals=size
        ),
    )(queries, kv0, kv0, kv1, kv1, query_rank, rank0, rank1, log_total, grad)


def shards(
    tokens,
    block_order,
    first_gain,
    first_shift,
    qkv_weight,
    query_value_bias,
    output_weight,
    output_bias,
    second_gain,
    second_shift,
    up_weight,
    up_bias,
    down_weight,
    down_bias,
    cotangent,
):
    R, G = lax.axis_size("row"), lax.axis_size("dp")
    r, c, g = lax.axis_index("row"), lax.axis_index("col"), lax.axis_index("dp")
    low = c == 0
    db, T = tokens.shape
    tq = T // R
    hp = HEADS // R
    W = hp * HEAD_DIM
    E = HEADS * HEAD_DIM - W * R
    X = E // HEAD_DIM
    half = W // 2
    pw = max(half, 2 * E)
    sub = up_weight.shape[1] // R
    GH = G // 2
    hr = db // GH

    def pad(values):
        return jnp.pad(values, ((0, 0), (0, pw - values.shape[1])))

    side = qkv_weight.shape[1] - D
    own_part = cut(qkv_weight, c * side, D, 1)
    own_keys = cut(qkv_weight, (1 - c) * D, side, 1)
    other_keys = swap(own_keys, "col", 1)
    key_part = jnp.concatenate(
        [jnp.where(low, own_keys, other_keys), jnp.where(low, other_keys, own_keys)], 1
    )
    source = jnp.where(g == 3, key_part, own_part)
    extra_keys = jnp.where(low, key_part[:, R * W :], 0)
    extras = pad(jnp.concatenate([own_part[:, R * W :], extra_keys], 1))
    offset = jnp.where(g == 3, c, g & 1) * half
    chunks = [
        jnp.where(g == 2, extras, pad(cut(source, (r ^ k) * W + offset, half, 1)))
        for k in range(R)
    ]
    piece = jnp.concatenate(trade(chunks, "row"), 0)
    x = jnp.concatenate(
        gather_near(tokens, "row", lambda sent: after(sent, piece[D - db :])), 0
    ).astype(f32)
    vectors = jnp.concatenate(
        gather_near(
            jnp.stack([first_gain, first_shift, output_bias, second_gain, second_shift]), "row"
        ),
        1,
    )
    g1, s1, ob, g2, s2 = [vectors[i][:, None] for i in range(5)]

    own_w = jnp.concatenate(settle(spread(piece, "dp"), g), 1)
    other_w = swap(own_w, "col", 1)
    lo, hi = jnp.where(low, own_w, other_w), jnp.where(low, other_w, own_w)
    wqkv = jnp.concatenate([lo, hi], 1)
    HW = W + E
    ex = 2 * pw
    kk = 3 * pw
    end = 4 * pw

    def arrange(main, main_x, extra_k, main_k):
        def fill(values):
            return jnp.pad(values, ((0, pw - values.shape[0]), (0, 0)))

        return [
            fill(main[:half]),
            fill(main[half:]),
            fill(jnp.concatenate([main_x, extra_k], 0)),
            fill(main_k),
        ]

    def bias_rows(values):
        nothing = jnp.zeros((E, 1), f32)
        return arrange(cut(values, r * W, W, 0), values[R * W :], nothing, nothing)

    bias = jnp.concatenate(
        [p for i in (0, 1) for p in bias_rows(query_value_bias[i][:, None])], 0
    )

    block = T * 2 // block_order.shape[1]
    places = (
        block_order.reshape(-1)[:, None] * block + jnp.arange(block, dtype=jnp.int32)[None, :]
    ).reshape(-1)
    own_places = cut(places, c * T, T, 0)
    other_places = cut(places, (1 - c) * T, T, 0)
    rank0, rank1 = own_places[:, None], other_places[:, None]
    query_rank = own_places[None, :]
    extra_rank = cut(query_rank, r * tq, tq, 1)

    normed1, n1, inv1 = norm_forward(x, g1, s1)
    projected = (dot(wqkv, normed1, 0, 0) + bias).astype(bf16)

    def rows_of(at, size):
        return projected[at : at + size]

    queries = jnp.concatenate([rows_of(0, half), rows_of(pw, half)], 0)
    queries_x = cut(rows_of(ex, E), r * tq, tq, 1)
    kv0 = jnp.concatenate(
        [
            rows_of(kk, half),
            rows_of(end + kk, half),
            rows_of(ex + E, E),
            rows_of(end, half),
            rows_of(end + pw, half),
            rows_of(end + ex, E),
        ],
        0,
    )
    kv1 = swap(kv0, "col", 1)
    outx, log_x = attend(queries_x, kv0, kv1, extra_rank, rank0, rank1, hp)
    out, log_main = attend(queries, kv0, kv1, query_rank, rank0, rank1, 0)
    part = jnp.where(
        g < GH,
        cut(up_weight, (g % GH) * hr, hr, 0),
        cut(down_weight, (g % GH) * hr, hr, 0),
    )
    part_o = cut(output_weight, g * (output_weight.shape[0] // G), output_weight.shape[0] // G, 0)
    part = after(part, x[D - db :])
    pieces = trade(
        [
            jnp.concatenate([cut(part, (r ^ k) * sub, sub, 1), part_o], 1)
            if hr == part_o.shape[0]
            else cut(part, (r ^ k) * sub, sub, 1)
            for k in range(R)
        ],
        "row",
    )
    if hr == part_o.shape[0]:
        part = jnp.stack(pieces)
        part = after(part, kv1)
        both = jnp.concatenate(
            [
                gather_placed(part[: R // 2], "dp", g, (2, 1), lambda v: after(v, out)),
                gather_placed(part[R // 2 :], "dp", g, (1, 2), lambda v: after(v, out)),
            ],
            1,
        )
        own_f, own_o = both[..., :sub], both[..., sub:]
    else:
        own_f = lax.all_gather(jnp.stack(pieces), "dp")
        own_o = lax.all_gather(jnp.stack(gather_near(part_o[None], "row")), "dp")
        own_o = own_o.reshape(G, R, part_o.shape[0], db)
    own_up, own_dn = [
        plain(
            jnp.concatenate([half_f[i, k] for k in range(R) for i in range(GH)], 0)
        )
        for half_f in (own_f[:GH], own_f[GH:])
    ]
    own_o = jnp.concatenate([own_o[:, k].reshape(-1, db) for k in range(R)], 1)
    other_o = swap(own_o, "col", 1)
    wo = jnp.concatenate([jnp.where(low, own_o, other_o), jnp.where(low, other_o, own_o)], 0)

    def swap_rows(values):
        return swap(values.reshape(R * GH, hr, sub), "col", 1).reshape(D, sub)

    other_up, other_dn = swap_rows(own_up), swap_rows(own_dn)
    own_ub = cut(up_bias, r * sub, sub, 0)
    other_ub = swap(own_ub, "col", 1)[None, :]
    own_ub = own_ub[None, :]

    packed = jnp.concatenate([out, outx.reshape(E // R, T)], 0)
    rows = gather_placed(packed, "row", r, bits(R))
    attended = jnp.concatenate(
        [
            rows[:, :W].reshape(R * W, T),
            rows[:, W:].reshape(R, E, tq).transpose(1, 0, 2).reshape(E, T),
        ],
        0,
    )
    middle = x + dot(wo, attended, 0, 0) + ob
    normed2, n2, inv2 = norm_forward(middle, g2, s2)

    hidden_a, slope_a = gelu_pair(dot(normed2, own_up, 0, 0) + own_ub)
    hidden_b, slope_b = gelu_pair(dot(normed2, other_up, 0, 0) + other_ub)

    upstream = jnp.concatenate(
        gather_near(after(cotangent, projected), "row", lambda sent: after(sent, out)), 0
    )
    before_a = (dot(upstream, own_dn, 0, 0) * slope_a).astype(bf16)
    before_b = (dot(upstream, other_dn, 0, 0) * slope_b).astype(bf16)
    part2 = dot(own_up, before_a, 1, 1) + dot(other_up, before_b, 1, 1)
    sg_part = jnp.sum(part2 * n2, 1)
    ss_part = jnp.sum(part2, 1)
    back2 = norm_backward(part2, n2, inv2, g2)
    away_up = plain(dot(normed2, before_b, 1, 0).astype(bf16))
    away_dn = plain(dot(upstream, hidden_b, 1, 0).astype(bf16))
    home_up = plain(dot(normed2, before_a, 1, 0))
    home_dn = plain(dot(upstream, hidden_a, 1, 0))
    mine = reduce_near(
        [cut(back2, (r ^ k) * tq, tq, 1) for k in range(R)],
        "row",
        lambda piece, bit: jnp.concatenate(
            [piece[(j ^ bit) * db : ((j ^ bit) + 1) * db] for j in range(R)], 0
        ),
        lambda sent: after(after(after(after(sent, away_up), away_dn), home_up), home_dn),
    )
    mine = mine + cut(upstream, r * tq, tq, 1).astype(f32)

    def col_sum(home, away):
        values = plain((home + swap_rows(away).astype(f32)).astype(bf16))
        return values.reshape(R, GH, hr, sub)

    down = dot(own_dn, hidden_a, 1, 1) + dot(other_dn, hidden_b, 1, 1)
    up_sum, dn_sum = col_sum(home_up, away_up), col_sum(home_dn, away_dn)
    which, part_high = (g & GH) != 0, (g & 1) != 0

    def by_weight(up, dn):
        arrived = swap(jnp.where(which, up, dn).astype(bf16), "dp", GH)
        return jnp.where(which, dn, up).astype(f32) + arrived.astype(f32), arrived

    def by_half(values):
        arrived = swap(
            jnp.where(part_high, values[..., 0, :, :], values[..., 1, :, :]).astype(bf16), "dp", 1
        )
        kept = jnp.where(part_high, values[..., 1, :, :], values[..., 0, :, :])
        return kept.astype(f32) + arrived.astype(f32)

    RH = R // 2
    first, stage = by_weight(up_sum[:RH], dn_sum[:RH])
    first = by_half(first)
    second, _ = by_weight(by_half(up_sum[RH:]), by_half(dn_sum[RH:]))
    branch = after(after(mine, down), up_sum.reshape(D, sub))
    branch = after(branch, dn_sum.reshape(D, sub)).astype(bf16)
    ob_part = jnp.sum(branch.astype(f32), 1)
    grad_att = dot(wo, branch, 1, 0).astype(bf16)
    go = jnp.concatenate(
        settle(trade([cut(grad_att, (r ^ k) * W, W, 0) for k in range(R)], "row"), r), 1
    )
    gox = grad_att[R * W :]
    branch_rows = jnp.concatenate(
        settle(trade(list(after(branch, go).reshape(R, db, tq)), "row"), r), 1
    )

    down = after(down, go)
    down = reduce_near([down[k * db : (k + 1) * db] for k in range(R)], "row")
    result = (middle[:db] + down + down_bias[:, None]).astype(bf16)

    both = jnp.concatenate([first, second], 0).astype(bf16)
    both = settle(trade(list(both), "row"), r)
    wide = R // 2 * sub
    both = jnp.concatenate(both, 1)
    both = jnp.concatenate(
        [
            gather_placed(both[:, :wide], "dp", g, (2, 1)),
            gather_placed(both[:, wide:], "dp", g, (1, 2)),
        ],
        2,
    )
    up_weight_grad = both[:GH].reshape(db, -1).astype(f32)
    down_weight_grad = both[GH:].reshape(db, -1).astype(f32)

    dwo = dot(attended, branch_rows, 1, 1)
    side_rows = dwo.shape[0] // 2
    lo_o, hi_o = dwo[:side_rows], dwo[side_rows:]
    arrived = swap(jnp.where(low, hi_o, lo_o).astype(bf16), "col", 1)
    mine_o = (jnp.where(low, lo_o, hi_o) + arrived.astype(f32)).astype(bf16)
    mine_o = mine_o.reshape(G, side_rows // G, db)
    mine_o = reduce_placed(mine_o, "dp", g, (1, 2)).astype(bf16)
    output_weight_grad = (
        gather_placed(mine_o, "dp", g, (2, 1)).reshape(side_rows, db).astype(f32)
    )

    gqx, *gx = attend_back(
        queries_x, kv0, kv1, extra_rank, rank0, rank1, hp, log_x, gox
    )
    gq, *gm = attend_back(queries, kv0, kv1, query_rank, rank0, rank1, 0, log_main, go)
    away = jnp.concatenate([gm[2], gx[2], gm[3], gx[3]], 0)
    arrived = swap(after(away, stage), "col", 1)
    gkv = (jnp.concatenate([gm[0], gx[0], gm[1], gx[1]], 0) + arrived.astype(f32)).astype(bf16)
    gqx = lax.dynamic_update_slice_in_dim(jnp.zeros((E, T), bf16), gqx, r * tq, 1)
    gk, gkx, gv, gvx = gkv[:W], gkv[W:HW], gkv[HW : HW + W], gkv[HW + W :]
    grad_p = jnp.concatenate(
        arrange(gq, gqx, gkx, gk[:half]) + arrange(gv, gvx, gkx, gk[half:]), 0
    )
    sums = jnp.sum(grad_p.astype(f32), 1)
    dw = dot(normed1, grad_p, 1, 1)
    lo_w, hi_w = dw[:, :end], dw[:, end:]
    arrived = swap(jnp.where(low, hi_w, lo_w).astype(bf16), "col", 1)
    mine_w = (jnp.where(low, lo_w, hi_w) + arrived.astype(f32)).astype(bf16)
    part1 = dot(wqkv, grad_p, 1, 0)
    fg_part = jnp.sum(part1 * n1, 1)
    fs_part = jnp.sum(part1, 1)
    back1 = norm_backward(part1, n1, inv1, after(g1, arrived))
    back1 = reduce_near([back1[k * db : (k + 1) * db] for k in range(R)], "row")
    input_grad = branch_rows.astype(f32) + back1

    mine_w = total(
        trade([cut(mine_w, (g ^ k) * pw, pw, 1) for k in range(G)], "dp")
    ).astype(bf16)
    mine_w = jnp.stack(settle(trade(list(mine_w.reshape(R, db, pw)), "row"), r))
    parts = settle(spread(mine_w, "dp"), g)
    ends = total([parts[2][i] for i in range(R)]).astype(bf16)
    mains = [p[:, :half] for i in range(R) for p in (parts[0][i], parts[1][i])]
    keys_own = jnp.stack([parts[3][i][:, :half] for i in range(R)])
    keys_other = swap(keys_own, "col", 1)
    keys_lo = jnp.where(low, keys_own, keys_other)
    keys_hi = jnp.where(low, keys_other, keys_own)
    keys_grad = jnp.concatenate(
        [p for i in range(R) for p in (keys_lo[i], keys_hi[i])] + [ends[:, E : 2 * E]], 1
    )
    main_grad = jnp.concatenate(mains + [ends[:, :E]], 1)
    qkv_weight_grad = jnp.where(
        low,
        jnp.concatenate([main_grad, keys_grad[:, :side]], 1),
        jnp.concatenate([keys_grad[:, D - side :], main_grad], 1),
    ).astype(f32)

    rel = jnp.stack([fg_part, fs_part, ob_part, sg_part, ss_part])
    rel = jnp.concatenate(settle(jnp.split(rel, R, 1), r), 1)

    def widen(values, width, start):
        return lax.dynamic_update_slice_in_dim(jnp.zeros((width,), f32), values, start, 0)

    db_part = widen(jnp.sum(cotangent.astype(f32), 1), D, r * db)

    def placed(at):
        main = jnp.concatenate([sums[at : at + half], sums[at + pw : at + pw + half]])
        return jnp.concatenate([widen(main, R * W, r * W), sums[at + ex : at + ex + E]])

    sum_a = jnp.sum(before_a.astype(f32), 0)
    sum_b = jnp.sum(before_b.astype(f32), 0)
    full = up_bias.shape[0]
    ub_part = widen(sum_a, 2 * full, c * full + r * sub) + widen(
        sum_b, 2 * full, (1 - c) * full + r * sub
    )
    small = jnp.concatenate(
        [
            rel,
            db_part[None],
            placed(0)[None],
            placed(end)[None],
            ub_part.reshape(-1, D),
        ],
        0,
    )
    for axis in ("col", "row", "dp"):
        k = 1
        while k < lax.axis_size(axis):
            small = small + swap(small, axis, k)
            k *= 2
    return (
        result,
        input_grad,
        small[0],
        small[1],
        qkv_weight_grad,
        small[6:8],
        output_weight_grad,
        small[2],
        small[3],
        small[4],
        up_weight_grad,
        small[8:].reshape(-1),
        down_weight_grad,
        small[5],
    )


def solution(mesh):
    placed = (
        P("row", ("dp", "col")),
        P("dp", None),
        P("row"),
        P("row"),
        P("row", "col"),
        P(),
        P("col", "row"),
        P("row"),
        P("row"),
        P("row"),
        P("row", "col"),
        P("col"),
        P("row", "col"),
        P("row"),
        P("row", ("dp", "col")),
    )
    return jax.shard_map(
        shards,
        mesh=mesh,
        in_specs=placed,
        out_specs=(
            P("row", ("dp", "col")),
            P("row", ("dp", "col")),
            P(),
            P(),
            P("row", "col"),
            P(),
            P("col", "row"),
            P(),
            P(),
            P(),
            P("row", "col"),
            P(),
            P("row", "col"),
            P(),
        ),
        check_vma=False,
    )
```

```python
import jax
import jax.numpy as jnp
from jax import lax
from jax.experimental import pallas as pl
from jax.experimental.layout import Layout, with_layout_constraint
from jax.experimental.pallas import tpu as pltpu
from jax.sharding import PartitionSpec as P

D = 1088
HEADS = 17
HEAD_DIM = 64
FF = 4352
epsilon = 1e-05
f32 = jnp.float32
bf16 = jnp.bfloat16


def gelu_pair(before):
    below = 0.5 + 0.5 * lax.erf(before * 0.5**0.5)
    density = jnp.exp(-0.5 * before * before) * (0.5 / jnp.pi) ** 0.5
    return (before * below).astype(bf16), below + before * density


def dot(left, right, left_dim, right_dim):
    return lax.dot_general(
        left, right, (((left_dim,), (right_dim,)), ((), ())), preferred_element_type=f32
    )


def plain(values):
    return with_layout_constraint(values, Layout(tuple(range(values.ndim))))


def swap(values, axis, k):
    pairs = [(i, i ^ k) for i in range(lax.axis_size(axis))]
    return plain(lax.ppermute(plain(values), axis, pairs))


def spread(values, axis):
    return [values] + [swap(values, axis, k) for k in range(1, lax.axis_size(axis))]


def trade(pieces, axis):
    return [pieces[0]] + [swap(pieces[k], axis, k) for k in range(1, len(pieces))]


def bits(count):
    out = []
    bit = count // 2
    while bit:
        out.append(bit)
        bit //= 2
    return out


def after(values, other):
    first = lax.slice(other, (0,) * other.ndim, (1,) * other.ndim).reshape(())
    return values + (first.astype(f32) * 0.0).astype(values.dtype)


def gather_near(values, axis, hold=None):
    got = {0: values}
    rows = values.shape[0]
    for bit in bits(lax.axis_size(axis)):
        names = sorted(got)
        sent = jnp.concatenate([got[k] for k in names], 0)
        if hold is not None and len(names) > 1:
            sent = hold(sent)
        arrived = swap(sent, axis, bit)
        for i, k in enumerate(names):
            got[k ^ bit] = arrived[i * rows : (i + 1) * rows]
    return [got[k] for k in range(len(got))]


def reduce_near(pieces, axis, regroup=None, hold=None, seen=None):
    left = dict(enumerate(pieces))
    rows = pieces[0].shape[0]
    for bit in bits(len(pieces))[::-1]:
        names = [k for k in sorted(left) if k & bit]
        sent = [left.pop(k) for k in names]
        if regroup is not None:
            sent = [regroup(piece, bit) for piece in sent]
        sent = jnp.concatenate(sent, 0).astype(bf16)
        if hold is not None and len(names) == 1:
            sent = hold(sent)
        arrived = swap(sent, axis, bit)
        if seen is not None:
            seen.append(arrived)
        for i, k in enumerate(names):
            left[k ^ bit] = left[k ^ bit] + arrived[i * rows : (i + 1) * rows].astype(f32)
    return left[0]


def gather_placed(values, axis, index, order, hold=None):
    done = []
    for bit in order:
        if hold is not None and done:
            values = hold(values)
        other = swap(values, axis, bit)
        high = (index & bit) != 0
        values = jnp.stack(
            [jnp.where(high, other, values), jnp.where(high, values, other)],
            sum(1 for b in done if b > bit),
        )
        done.append(bit)
    return values.reshape((-1,) + values.shape[len(done) :])


def reduce_placed(values, axis, index, order, steps=False):
    count = lax.axis_size(axis)
    names = bits(count)
    values = values.reshape((2,) * len(names) + values.shape[1:])
    for bit in order:
        place = names.index(bit)
        zero, one = [lax.index_in_dim(values, i, place, False) for i in (0, 1)]
        high = (index & bit) != 0
        arrived = swap(jnp.where(high, zero, one).astype(bf16), axis, bit)
        values = jnp.where(high, one, zero).astype(f32) + arrived.astype(f32)
        names.remove(bit)
        if steps and bit == order[0]:
            stage = arrived
    return (values, stage) if steps else values


def settle(pieces, index):
    pieces = list(pieces)
    bit = 1
    while bit < len(pieces):
        odd = (index & bit) != 0
        pieces = [jnp.where(odd, pieces[k ^ bit], pieces[k]) for k in range(len(pieces))]
        bit *= 2
    return pieces


def total(pieces):
    out = pieces[0].astype(f32)
    for piece in pieces[1:]:
        out = out + piece.astype(f32)
    return out


def cut(values, start, size, dim):
    return lax.dynamic_slice_in_dim(values, start, size, dim)


def norm_forward(rows, gain, shift):
    average = jnp.sum(rows, 0, keepdims=True) / D
    centered = rows - average
    variance = jnp.sum(centered * centered, 0, keepdims=True) / D
    inverse = lax.rsqrt(variance + epsilon)
    normal = centered * inverse
    return (normal * gain + shift).astype(bf16), normal, inverse


def norm_backward(upstream, normal, inverse, gain):
    scaled = upstream * gain
    first = jnp.sum(scaled, 0, keepdims=True) / D
    second = jnp.sum(scaled * normal, 0, keepdims=True) / D
    return inverse * (scaled - first - normal * second)


SCALE = HEAD_DIM ** (-0.5)


def masked(keys, scaled, key_rank, query_rank):
    scores = dot(keys, scaled, 0, 0)
    return jnp.where(key_rank <= query_rank, scores, -1e30)


def attend_kernel(q, k0, v0, k1, v1, query_rank, rank0, rank1, out, log_total):
    scaled = q[...] * jnp.asarray(SCALE, bf16)
    query = query_rank[...]
    s0 = masked(k0[...], scaled, rank0[...], query)
    s1 = masked(k1[...], scaled, rank1[...], query)
    largest = jnp.maximum(jnp.max(s0, 0, keepdims=True), jnp.max(s1, 0, keepdims=True))
    p0 = jnp.exp(s0 - largest)
    p1 = jnp.exp(s1 - largest)
    totals = jnp.sum(p0, 0, keepdims=True) + jnp.sum(p1, 0, keepdims=True)
    got = dot(v0[...], p0.astype(bf16), 1, 0) + dot(v1[...], p1.astype(bf16), 1, 0)
    out[...] = (got / totals).astype(bf16)
    log_total[...] = (largest + jnp.log(totals))[None]


def back_kernel(
    q, k0, v0, k1, v1, query_rank, rank0, rank1, log_total, grad, gq, gk0, gv0, gk1, gv1, sums
):
    step = pl.program_id(1)

    @pl.when(step == 0)
    def _():
        sums[...] = jnp.zeros_like(sums)

    scaled = q[...] * jnp.asarray(SCALE, bf16)
    query = query_rank[...]
    shift = log_total[...][0]
    g = grad[...]
    p0 = jnp.exp(masked(k0[...], scaled, rank0[...], query) - shift)
    p1 = jnp.exp(masked(k1[...], scaled, rank1[...], query) - shift)
    w0 = dot(v0[...], g, 0, 0)
    w1 = dot(v1[...], g, 0, 0)
    inner = jnp.sum(p0 * w0, 0, keepdims=True) + jnp.sum(p1 * w1, 0, keepdims=True)
    d0 = (p0 * (w0 - inner)).astype(bf16)
    d1 = (p1 * (w1 - inner)).astype(bf16)
    gq[...] = ((dot(k0[...], d0, 1, 0) + dot(k1[...], d1, 1, 0)) * SCALE).astype(gq.dtype)
    sums[0] += dot(scaled, d0, 1, 1)
    sums[1] += dot(g, p0.astype(bf16), 1, 1)
    sums[2] += dot(scaled, d1, 1, 1)
    sums[3] += dot(g, p1.astype(bf16), 1, 1)

    @pl.when(step == pl.num_programs(1) - 1)
    def _():
        gk0[...] = sums[0].astype(gk0.dtype)
        gv0[...] = sums[1].astype(gv0.dtype)
        gk1[...] = sums[2].astype(gk1.dtype)
        gv1[...] = sums[3].astype(gv1.dtype)


def attention_specs(width, T, first, all_heads):
    def key_spec(at):
        return pl.BlockSpec((HEAD_DIM, T), lambda h, i: (at + h, 0))

    row = pl.BlockSpec((HEAD_DIM, width), lambda h, i: (h, i))
    ranks = [pl.BlockSpec((1, width), lambda h, i: (0, i))] + [
        pl.BlockSpec((T, 1), lambda h, i: (0, 0))
    ] * 2
    pair = [key_spec(first), key_spec(all_heads + first)]
    return row, [row] + pair + pair + ranks


def attend(queries, kv0, kv1, query_rank, rank0, rank1, first):
    heads, t = queries.shape[0] // HEAD_DIM, queries.shape[1]
    T = kv0.shape[1]
    width = min(t, 512)
    row, specs = attention_specs(width, T, first, kv0.shape[0] // HEAD_DIM // 2)
    size = heads * t * 2 * T
    return pl.pallas_call(
        attend_kernel,
        grid=(heads, t // width),
        in_specs=specs,
        out_specs=[row, pl.BlockSpec((1, 1, width), lambda h, i: (h, 0, i))],
        out_shape=[
            jax.ShapeDtypeStruct(queries.shape, bf16),
            jax.ShapeDtypeStruct((heads, 1, t), f32),
        ],
        compiler_params=pltpu.CompilerParams(vmem_limit_bytes=40 * 2**20),
        cost_estimate=pl.CostEstimate(
            flops=size * 4 * HEAD_DIM * 4, bytes_accessed=4 * kv0.size, transcendentals=size
        ),
    )(queries, kv0, kv0, kv1, kv1, query_rank, rank0, rank1)


def attend_back(queries, kv0, kv1, query_rank, rank0, rank1, first, log_total, grad):
    heads, t = queries.shape[0] // HEAD_DIM, queries.shape[1]
    T = kv0.shape[1]
    width = min(t, 512)
    row, specs = attention_specs(width, T, first, kv0.shape[0] // HEAD_DIM // 2)
    size = heads * t * 2 * T
    grads = pl.BlockSpec((HEAD_DIM, T), lambda h, i: (h, 0))
    return pl.pallas_call(
        back_kernel,
        grid=(heads, t // width),
        in_specs=specs + [pl.BlockSpec((1, 1, width), lambda h, i: (h, 0, i)), row],
        out_specs=[row] + [grads] * 4,
        out_shape=[jax.ShapeDtypeStruct(queries.shape, bf16)]
        + [jax.ShapeDtypeStruct((heads * HEAD_DIM, T), d) for d in (f32, f32, bf16, bf16)],
        scratch_shapes=[pltpu.VMEM((4, HEAD_DIM, T), f32)],
        compiler_params=pltpu.CompilerParams(vmem_limit_bytes=48 * 2**20),
        cost_estimate=pl.CostEstimate(
            flops=size * 10 * HEAD_DIM * 4, bytes_accessed=8 * kv0.size, transcendentals=size
        ),
    )(queries, kv0, kv0, kv1, kv1, query_rank, rank0, rank1, log_total, grad)


def shards(
    tokens,
    block_order,
    first_gain,
    first_shift,
    qkv_weight,
    query_value_bias,
    output_weight,
    output_bias,
    second_gain,
    second_shift,
    up_weight,
    up_bias,
    down_weight,
    down_bias,
    cotangent,
):
    R, G = lax.axis_size("row"), lax.axis_size("dp")
    r, c, g = lax.axis_index("row"), lax.axis_index("col"), lax.axis_index("dp")
    low = c == 0
    db, T = tokens.shape
    tq = T // R
    hp = HEADS // R
    W = hp * HEAD_DIM
    E = HEADS * HEAD_DIM - W * R
    X = E // HEAD_DIM
    half = W // 2
    pw = max(half, 2 * E)
    sub = up_weight.shape[1] // R
    GH = G // 2
    hr = db // GH

    def pad(values):
        return jnp.pad(values, ((0, 0), (0, pw - values.shape[1])))

    side = qkv_weight.shape[1] - D
    own_part = cut(qkv_weight, c * side, D, 1)
    own_keys = cut(qkv_weight, (1 - c) * D, side, 1)
    other_keys = swap(own_keys, "col", 1)
    key_part = jnp.concatenate(
        [jnp.where(low, own_keys, other_keys), jnp.where(low, other_keys, own_keys)], 1
    )
    source = jnp.where(g == 3, key_part, own_part)
    extra_keys = jnp.where(low, key_part[:, R * W :], 0)
    extras = pad(jnp.concatenate([own_part[:, R * W :], extra_keys], 1))
    offset = jnp.where(g == 3, c, g & 1) * half
    chunks = [
        jnp.where(g == 2, extras, pad(cut(source, (r ^ k) * W + offset, half, 1)))
        for k in range(R)
    ]
    piece = jnp.concatenate(trade(chunks, "row"), 0)
    x = jnp.concatenate(
        gather_near(tokens, "row", lambda sent: after(sent, piece[D - db :])), 0
    ).astype(f32)
    vectors = jnp.concatenate(
        gather_near(
            jnp.stack([first_gain, first_shift, output_bias, second_gain, second_shift]), "row"
        ),
        1,
    )
    g1, s1, ob, g2, s2 = [vectors[i][:, None] for i in range(5)]

    own_w = jnp.concatenate(settle(spread(piece, "dp"), g), 1)
    other_w = swap(own_w, "col", 1)
    lo, hi = jnp.where(low, own_w, other_w), jnp.where(low, other_w, own_w)
    wqkv = jnp.concatenate([lo, hi], 1)
    HW = W + E
    ex = 2 * pw
    kk = 3 * pw
    end = 4 * pw

    def arrange(main, main_x, extra_k, main_k):
        def fill(values):
            return jnp.pad(values, ((0, pw - values.shape[0]), (0, 0)))

        return [
            fill(main[:half]),
            fill(main[half:]),
            fill(jnp.concatenate([main_x, extra_k], 0)),
            fill(main_k),
        ]

    def bias_rows(values):
        nothing = jnp.zeros((E, 1), f32)
        return arrange(cut(values, r * W, W, 0), values[R * W :], nothing, nothing)

    bias = jnp.concatenate(
        [p for i in (0, 1) for p in bias_rows(query_value_bias[i][:, None])], 0
    )

    block = T * 2 // block_order.shape[1]
    places = (
        block_order.reshape(-1)[:, None] * block + jnp.arange(block, dtype=jnp.int32)[None, :]
    ).reshape(-1)
    own_places = cut(places, c * T, T, 0)
    other_places = cut(places, (1 - c) * T, T, 0)
    rank0, rank1 = own_places[:, None], other_places[:, None]
    query_rank = own_places[None, :]
    extra_rank = cut(query_rank, r * tq, tq, 1)

    normed1, n1, inv1 = norm_forward(x, g1, s1)
    projected = (dot(wqkv, normed1, 0, 0) + bias).astype(bf16)

    def rows_of(at, size):
        return projected[at : at + size]

    queries = jnp.concatenate([rows_of(0, half), rows_of(pw, half)], 0)
    queries_x = cut(rows_of(ex, E), r * tq, tq, 1)
    kv0 = jnp.concatenate(
        [
            rows_of(kk, half),
            rows_of(end + kk, half),
            rows_of(ex + E, E),
            rows_of(end, half),
            rows_of(end + pw, half),
            rows_of(end + ex, E),
        ],
        0,
    )
    kv1 = swap(kv0, "col", 1)
    outx, log_x = attend(queries_x, kv0, kv1, extra_rank, rank0, rank1, hp)
    out, log_main = attend(queries, kv0, kv1, query_rank, rank0, rank1, 0)
    part = jnp.where(
        g < GH,
        cut(up_weight, (g % GH) * hr, hr, 0),
        cut(down_weight, (g % GH) * hr, hr, 0),
    )
    part_o = cut(output_weight, g * (output_weight.shape[0] // G), output_weight.shape[0] // G, 0)
    part = after(part, piece[D - db :])
    pieces = trade([cut(part, (r ^ k) * sub, sub, 1) for k in range(R)], "row")
    piece_o = jnp.concatenate(
        gather_near(after(part_o, piece[D - db :]), "row", lambda v: after(v, kv1)), 1
    )
    part = after(jnp.stack(pieces), kv1)
    which, part_high = (g & GH) != 0, (g & 1) != 0

    def both_weights(values):
        other = swap(values, "dp", GH)
        return jnp.stack(
            [jnp.where(which, other, values), jnp.where(which, values, other)], 0
        )

    def both_halves(values):
        other = swap(values, "dp", 1)
        return jnp.stack(
            [jnp.where(part_high, other, values), jnp.where(part_high, values, other)], -3
        )

    RH = R // 2
    front = both_halves(after(both_weights(part[:RH]), out))
    back = both_weights(after(both_halves(part[RH:]), out))
    own_up, own_dn = [
        plain(jnp.concatenate([front[i], back[i]], 0).reshape(D, sub)) for i in (0, 1)
    ]
    own_o = gather_placed(piece_o, "dp", g, (2, 1), lambda v: after(v, out)).reshape(-1, D)
    other_o = swap(own_o, "col", 1)
    wo = jnp.concatenate([jnp.where(low, own_o, other_o), jnp.where(low, other_o, own_o)], 0)

    def swap_rows(values):
        return swap(values.reshape(R * GH, hr, sub), "col", 1).reshape(D, sub)

    other_up, other_dn = swap_rows(own_up), swap_rows(own_dn)
    own_ub = cut(up_bias, r * sub, sub, 0)
    other_ub = swap(own_ub, "col", 1)[None, :]
    own_ub = own_ub[None, :]

    packed = jnp.concatenate([out, outx.reshape(E // R, T)], 0)
    seen = []

    def watch(values):
        seen.append(values)
        return values

    rows = gather_placed(packed, "row", r, bits(R), watch)
    attended = jnp.concatenate(
        [
            rows[:, :W].reshape(R * W, T),
            rows[:, W:].reshape(R, E, tq).transpose(1, 0, 2).reshape(E, T),
        ],
        0,
    )
    middle = x + dot(wo, attended, 0, 0) + ob
    normed2, n2, inv2 = norm_forward(middle, g2, s2)

    hidden_a, slope_a = gelu_pair(dot(normed2, own_up, 0, 0) + own_ub)
    hidden_b, slope_b = gelu_pair(dot(normed2, other_up, 0, 0) + other_ub)

    upstream = jnp.concatenate(
        gather_near(after(cotangent, seen[0]), "row", lambda sent: after(sent, rows)), 0
    )
    before_a = (dot(upstream, own_dn, 0, 0) * slope_a).astype(bf16)
    before_b = (dot(upstream, other_dn, 0, 0) * slope_b).astype(bf16)
    part2 = dot(own_up, before_a, 1, 1) + dot(other_up, before_b, 1, 1)
    sg_part = jnp.sum(part2 * n2, 1)
    ss_part = jnp.sum(part2, 1)
    back2 = norm_backward(part2, n2, inv2, g2)
    away_up = plain(dot(normed2, before_b, 1, 0).astype(bf16))
    away_dn = plain(dot(upstream, hidden_b, 1, 0).astype(bf16))
    home_up = plain(dot(normed2, before_a, 1, 0))
    home_dn = plain(dot(upstream, hidden_a, 1, 0))
    seen2 = []
    mine = reduce_near(
        [cut(back2, (r ^ k) * tq, tq, 1) for k in range(R)],
        "row",
        lambda piece, bit: jnp.concatenate(
            [piece[(j ^ bit) * db : ((j ^ bit) + 1) * db] for j in range(R)], 0
        ),
        None,
        seen2,
    )
    mine = mine + cut(upstream, r * tq, tq, 1).astype(f32)

    def col_sum(home, away):
        values = home + swap_rows(away).astype(f32)
        values = plain(after(values, seen2[0]).astype(bf16))
        return values.reshape(R, GH, hr, sub)

    down = dot(own_dn, hidden_a, 1, 1) + dot(other_dn, hidden_b, 1, 1)
    down = after(down, seen2[0])
    up_sum, dn_sum = col_sum(home_up, away_up), col_sum(home_dn, away_dn)
    def by_weight(up, dn):
        arrived = swap(jnp.where(which, up, dn).astype(bf16), "dp", GH)
        return jnp.where(which, dn, up).astype(f32) + arrived.astype(f32), arrived

    def by_half(values):
        arrived = swap(
            jnp.where(part_high, values[..., 0, :, :], values[..., 1, :, :]).astype(bf16), "dp", 1
        )
        kept = jnp.where(part_high, values[..., 1, :, :], values[..., 0, :, :])
        return kept.astype(f32) + arrived.astype(f32)

    first, stage = by_weight(up_sum[:RH], dn_sum[:RH])
    second_up, second_dn = by_half(up_sum[RH:]), by_half(dn_sum[RH:])

    branch = mine.astype(bf16)
    ob_part = jnp.sum(branch.astype(f32), 1)
    grad_att = dot(wo, branch, 1, 0).astype(bf16)
    go = jnp.concatenate(
        settle(trade([cut(grad_att, (r ^ k) * W, W, 0) for k in range(R)], "row"), r), 1
    )
    gox = grad_att[R * W :]
    log_main = after(after(log_main, up_sum), dn_sum)
    gqx, *gx = attend_back(
        queries_x, kv0, kv1, extra_rank, rank0, rank1, hp, log_x, gox
    )
    gq, *gm = attend_back(queries, kv0, kv1, query_rank, rank0, rank1, 0, log_main, go)

    down = reduce_near(
        [down[k * db : (k + 1) * db] for k in range(R)],
        "row",
        None,
        lambda sent: after(sent, go),
    )

    away = jnp.concatenate([gm[2], gx[2], gm[3], gx[3]], 0)
    arrived = swap(away, "col", 1)
    gkv = (jnp.concatenate([gm[0], gx[0], gm[1], gx[1]], 0) + arrived.astype(f32)).astype(bf16)
    gqx = lax.dynamic_update_slice_in_dim(jnp.zeros((E, T), bf16), gqx, r * tq, 1)
    gk, gkx, gv, gvx = gkv[:W], gkv[W:HW], gkv[HW : HW + W], gkv[HW + W :]
    grad_p = jnp.concatenate(
        arrange(gq, gqx, gkx, gk[:half]) + arrange(gv, gvx, gkx, gk[half:]), 0
    )
    sums = jnp.sum(grad_p.astype(f32), 1)
    dw = dot(normed1, grad_p, 1, 1)
    lo_w, hi_w = dw[:, :end], dw[:, end:]
    arrived = swap(jnp.where(low, hi_w, lo_w).astype(bf16), "col", 1)
    mine_w = (jnp.where(low, lo_w, hi_w) + arrived.astype(f32)).astype(bf16)
    part1 = dot(wqkv, grad_p, 1, 0)
    fg_part = jnp.sum(part1 * n1, 1)
    fs_part = jnp.sum(part1, 1)
    back1 = norm_backward(part1, n1, inv1, after(g1, arrived))
    back1_low = back1.astype(bf16)

    mine_w = total(
        trade([cut(mine_w, (g ^ k) * pw, pw, 1) for k in range(G)], "dp")
    ).astype(bf16)
    back1 = reduce_near(
        [back1[k * db : (k + 1) * db] for k in range(R)],
        "row",
        None,
        lambda sent: after(sent, mine_w),
    )
    mine_w = jnp.stack(settle(trade(list(mine_w.reshape(R, db, pw)), "row"), r))
    parts = settle(spread(mine_w, "dp"), g)
    ends = total([parts[2][i] for i in range(R)]).astype(bf16)
    mains = [p[:, :half] for i in range(R) for p in (parts[0][i], parts[1][i])]
    keys_own = jnp.stack([parts[3][i][:, :half] for i in range(R)])
    keys_other = swap(keys_own, "col", 1)
    keys_lo = jnp.where(low, keys_own, keys_other)
    keys_hi = jnp.where(low, keys_other, keys_own)
    keys_grad = jnp.concatenate(
        [p for i in range(R) for p in (keys_lo[i], keys_hi[i])] + [ends[:, E : 2 * E]], 1
    )
    main_grad = jnp.concatenate(mains + [ends[:, :E]], 1)
    qkv_weight_grad = jnp.where(
        low,
        jnp.concatenate([main_grad, keys_grad[:, :side]], 1),
        jnp.concatenate([keys_grad[:, D - side :], main_grad], 1),
    ).astype(f32)

    first = by_half(after(first, back1_low))
    second, _ = by_weight(after(second_up, back1_low), second_dn)
    both = jnp.concatenate([first, second], 0).astype(bf16)
    both = settle(trade(list(both), "row"), r)
    wide = R // 2 * sub
    both = jnp.concatenate(both, 1)
    both = jnp.concatenate(
        [
            gather_placed(both[:, :wide], "dp", g, (2, 1)),
            gather_placed(both[:, wide:], "dp", g, (1, 2)),
        ],
        2,
    )
    up_weight_grad = both[:GH].reshape(db, -1).astype(f32)
    down_weight_grad = both[GH:].reshape(db, -1).astype(f32)

    branch_rows = jnp.concatenate(
        settle(trade(list(after(branch, back1_low).reshape(R, db, tq)), "row"), r), 1
    )
    result = (middle[:db] + after(down, back1_low) + down_bias[:, None]).astype(bf16)
    input_grad = branch_rows.astype(f32) + back1

    dwo = after(dot(attended, branch_rows, 1, 1), back1_low)
    side_rows = dwo.shape[0] // 2
    lo_o, hi_o = dwo[:side_rows], dwo[side_rows:]
    arrived = swap(jnp.where(low, hi_o, lo_o).astype(bf16), "col", 1)
    mine_o = (jnp.where(low, lo_o, hi_o) + arrived.astype(f32)).astype(bf16)
    mine_o = mine_o.reshape(G, side_rows // G, db)
    mine_o = reduce_placed(mine_o, "dp", g, (1, 2)).astype(bf16)
    output_weight_grad = (
        gather_placed(mine_o, "dp", g, (2, 1)).reshape(side_rows, db).astype(f32)
    )

    rel = jnp.stack([fg_part, fs_part, ob_part, sg_part, ss_part])
    rel = jnp.concatenate(settle(jnp.split(rel, R, 1), r), 1)

    def widen(values, width, start):
        return lax.dynamic_update_slice_in_dim(jnp.zeros((width,), f32), values, start, 0)

    db_part = widen(jnp.sum(cotangent.astype(f32), 1), D, r * db)

    def placed(at):
        main = jnp.concatenate([sums[at : at + half], sums[at + pw : at + pw + half]])
        return jnp.concatenate([widen(main, R * W, r * W), sums[at + ex : at + ex + E]])

    sum_a = jnp.sum(before_a.astype(f32), 0)
    sum_b = jnp.sum(before_b.astype(f32), 0)
    full = up_bias.shape[0]
    ub_part = widen(sum_a, 2 * full, c * full + r * sub) + widen(
        sum_b, 2 * full, (1 - c) * full + r * sub
    )
    small = jnp.concatenate(
        [
            rel,
            db_part[None],
            placed(0)[None],
            placed(end)[None],
            ub_part.reshape(-1, D),
        ],
        0,
    )
    for axis in ("col", "row", "dp"):
        k = 1
        while k < lax.axis_size(axis):
            small = small + swap(small, axis, k)
            k *= 2
    return (
        result,
        input_grad,
        small[0],
        small[1],
        qkv_weight_grad,
        small[6:8],
        output_weight_grad,
        small[2],
        small[3],
        small[4],
        up_weight_grad,
        small[8:].reshape(-1),
        down_weight_grad,
        small[5],
    )


def solution(mesh):
    placed = (
        P("row", ("dp", "col")),
        P("dp", None),
        P("row"),
        P("row"),
        P("row", "col"),
        P(),
        P("col", "row"),
        P("row"),
        P("row"),
        P("row"),
        P("row", "col"),
        P("col"),
        P("row", "col"),
        P("row"),
        P("row", ("dp", "col")),
    )
    return jax.shard_map(
        shards,
        mesh=mesh,
        in_specs=placed,
        out_specs=(
            P("row", ("dp", "col")),
            P("row", ("dp", "col")),
            P(),
            P(),
            P("row", "col"),
            P(),
            P("col", "row"),
            P(),
            P(),
            P(),
            P("row", "col"),
            P(),
            P("row", "col"),
            P(),
        ),
        check_vma=False,
    )
```

```python
import jax
import jax.numpy as jnp
from jax import lax
from jax.experimental import pallas as pl
from jax.experimental.layout import Layout, with_layout_constraint
from jax.experimental.pallas import tpu as pltpu
from jax.sharding import PartitionSpec as P

D = 1088
HEADS = 17
HEAD_DIM = 64
FF = 4352
epsilon = 1e-05
f32 = jnp.float32
bf16 = jnp.bfloat16


def gelu_pair(before):
    below = 0.5 + 0.5 * lax.erf(before * 0.5**0.5)
    density = jnp.exp(-0.5 * before * before) * (0.5 / jnp.pi) ** 0.5
    return (before * below).astype(bf16), below + before * density


def dot(left, right, left_dim, right_dim):
    return lax.dot_general(
        left, right, (((left_dim,), (right_dim,)), ((), ())), preferred_element_type=f32
    )


def plain(values):
    return with_layout_constraint(values, Layout(tuple(range(values.ndim))))


def swap(values, axis, k):
    pairs = [(i, i ^ k) for i in range(lax.axis_size(axis))]
    return plain(lax.ppermute(plain(values), axis, pairs))


def spread(values, axis):
    return [values] + [swap(values, axis, k) for k in range(1, lax.axis_size(axis))]


def trade(pieces, axis):
    return [pieces[0]] + [swap(pieces[k], axis, k) for k in range(1, len(pieces))]


def bits(count):
    out = []
    bit = count // 2
    while bit:
        out.append(bit)
        bit //= 2
    return out


def after(values, other):
    first = lax.slice(other, (0,) * other.ndim, (1,) * other.ndim).reshape(())
    return values + (first.astype(f32) * 0.0).astype(values.dtype)


def gather_near(values, axis, hold=None):
    got = {0: values}
    rows = values.shape[0]
    for bit in bits(lax.axis_size(axis)):
        names = sorted(got)
        sent = jnp.concatenate([got[k] for k in names], 0)
        if hold is not None and len(names) > 1:
            sent = hold(sent)
        arrived = swap(sent, axis, bit)
        for i, k in enumerate(names):
            got[k ^ bit] = arrived[i * rows : (i + 1) * rows]
    return [got[k] for k in range(len(got))]


def reduce_near(pieces, axis, regroup=None, hold=None, seen=None):
    left = dict(enumerate(pieces))
    rows = pieces[0].shape[0]
    for bit in bits(len(pieces))[::-1]:
        names = [k for k in sorted(left) if k & bit]
        sent = [left.pop(k) for k in names]
        if regroup is not None:
            sent = [regroup(piece, bit) for piece in sent]
        sent = jnp.concatenate(sent, 0).astype(bf16)
        if hold is not None and len(names) == 1:
            sent = hold(sent)
        arrived = swap(sent, axis, bit)
        if seen is not None:
            seen.append(arrived)
        for i, k in enumerate(names):
            left[k ^ bit] = left[k ^ bit] + arrived[i * rows : (i + 1) * rows].astype(f32)
    return left[0]


def gather_placed(values, axis, index, order, hold=None):
    done = []
    for bit in order:
        if hold is not None and done:
            values = hold(values)
        other = swap(values, axis, bit)
        high = (index & bit) != 0
        values = jnp.stack(
            [jnp.where(high, other, values), jnp.where(high, values, other)],
            sum(1 for b in done if b > bit),
        )
        done.append(bit)
    return values.reshape((-1,) + values.shape[len(done) :])


def reduce_placed(values, axis, index, order, steps=False):
    count = lax.axis_size(axis)
    names = bits(count)
    values = values.reshape((2,) * len(names) + values.shape[1:])
    for bit in order:
        place = names.index(bit)
        zero, one = [lax.index_in_dim(values, i, place, False) for i in (0, 1)]
        high = (index & bit) != 0
        arrived = swap(jnp.where(high, zero, one).astype(bf16), axis, bit)
        values = jnp.where(high, one, zero).astype(f32) + arrived.astype(f32)
        names.remove(bit)
        if steps and bit == order[0]:
            stage = arrived
    return (values, stage) if steps else values


def settle(pieces, index):
    pieces = list(pieces)
    bit = 1
    while bit < len(pieces):
        odd = (index & bit) != 0
        pieces = [jnp.where(odd, pieces[k ^ bit], pieces[k]) for k in range(len(pieces))]
        bit *= 2
    return pieces


def total(pieces):
    out = pieces[0].astype(f32)
    for piece in pieces[1:]:
        out = out + piece.astype(f32)
    return out


def cut(values, start, size, dim):
    return lax.dynamic_slice_in_dim(values, start, size, dim)


def norm_forward(rows, gain, shift):
    average = jnp.sum(rows, 0, keepdims=True) / D
    centered = rows - average
    variance = jnp.sum(centered * centered, 0, keepdims=True) / D
    inverse = lax.rsqrt(variance + epsilon)
    normal = centered * inverse
    return (normal * gain + shift).astype(bf16), normal, inverse


def norm_backward(upstream, normal, inverse, gain):
    scaled = upstream * gain
    first = jnp.sum(scaled, 0, keepdims=True) / D
    second = jnp.sum(scaled * normal, 0, keepdims=True) / D
    return inverse * (scaled - first - normal * second)


SCALE = HEAD_DIM ** (-0.5)


def masked(keys, scaled, key_rank, query_rank):
    scores = dot(keys, scaled, 0, 0)
    return jnp.where(key_rank <= query_rank, scores, -1e30)


def attend_kernel(q, k0, v0, k1, v1, query_rank, rank0, rank1, out, log_total):
    scaled = q[...] * jnp.asarray(SCALE, bf16)
    query = query_rank[...]
    s0 = masked(k0[...], scaled, rank0[...], query)
    s1 = masked(k1[...], scaled, rank1[...], query)
    largest = jnp.maximum(jnp.max(s0, 0, keepdims=True), jnp.max(s1, 0, keepdims=True))
    p0 = jnp.exp(s0 - largest)
    p1 = jnp.exp(s1 - largest)
    totals = jnp.sum(p0, 0, keepdims=True) + jnp.sum(p1, 0, keepdims=True)
    got = dot(v0[...], p0.astype(bf16), 1, 0) + dot(v1[...], p1.astype(bf16), 1, 0)
    out[...] = (got / totals).astype(bf16)
    log_total[...] = (largest + jnp.log(totals))[None]


def back_kernel(
    q, k0, v0, k1, v1, query_rank, rank0, rank1, log_total, grad, gq, gk0, gv0, gk1, gv1, sums
):
    step = pl.program_id(1)

    @pl.when(step == 0)
    def _():
        sums[...] = jnp.zeros_like(sums)

    scaled = q[...] * jnp.asarray(SCALE, bf16)
    query = query_rank[...]
    shift = log_total[...][0]
    g = grad[...]
    p0 = jnp.exp(masked(k0[...], scaled, rank0[...], query) - shift)
    p1 = jnp.exp(masked(k1[...], scaled, rank1[...], query) - shift)
    w0 = dot(v0[...], g, 0, 0)
    w1 = dot(v1[...], g, 0, 0)
    inner = jnp.sum(p0 * w0, 0, keepdims=True) + jnp.sum(p1 * w1, 0, keepdims=True)
    d0 = (p0 * (w0 - inner)).astype(bf16)
    d1 = (p1 * (w1 - inner)).astype(bf16)
    gq[...] = ((dot(k0[...], d0, 1, 0) + dot(k1[...], d1, 1, 0)) * SCALE).astype(gq.dtype)
    sums[0] += dot(scaled, d0, 1, 1)
    sums[1] += dot(g, p0.astype(bf16), 1, 1)
    sums[2] += dot(scaled, d1, 1, 1)
    sums[3] += dot(g, p1.astype(bf16), 1, 1)

    @pl.when(step == pl.num_programs(1) - 1)
    def _():
        gk0[...] = sums[0].astype(gk0.dtype)
        gv0[...] = sums[1].astype(gv0.dtype)
        gk1[...] = sums[2].astype(gk1.dtype)
        gv1[...] = sums[3].astype(gv1.dtype)


def attention_specs(width, T, first, all_heads):
    def key_spec(at):
        return pl.BlockSpec((HEAD_DIM, T), lambda h, i: (at + h, 0))

    row = pl.BlockSpec((HEAD_DIM, width), lambda h, i: (h, i))
    ranks = [pl.BlockSpec((1, width), lambda h, i: (0, i))] + [
        pl.BlockSpec((T, 1), lambda h, i: (0, 0))
    ] * 2
    pair = [key_spec(first), key_spec(all_heads + first)]
    return row, [row] + pair + pair + ranks


def attend(queries, kv0, kv1, query_rank, rank0, rank1, first):
    heads, t = queries.shape[0] // HEAD_DIM, queries.shape[1]
    T = kv0.shape[1]
    width = min(t, 512)
    row, specs = attention_specs(width, T, first, kv0.shape[0] // HEAD_DIM // 2)
    size = heads * t * 2 * T
    return pl.pallas_call(
        attend_kernel,
        grid=(heads, t // width),
        in_specs=specs,
        out_specs=[row, pl.BlockSpec((1, 1, width), lambda h, i: (h, 0, i))],
        out_shape=[
            jax.ShapeDtypeStruct(queries.shape, bf16),
            jax.ShapeDtypeStruct((heads, 1, t), f32),
        ],
        compiler_params=pltpu.CompilerParams(vmem_limit_bytes=40 * 2**20),
        cost_estimate=pl.CostEstimate(
            flops=size * 4 * HEAD_DIM * 4, bytes_accessed=4 * kv0.size, transcendentals=size
        ),
    )(queries, kv0, kv0, kv1, kv1, query_rank, rank0, rank1)


def attend_back(queries, kv0, kv1, query_rank, rank0, rank1, first, log_total, grad):
    heads, t = queries.shape[0] // HEAD_DIM, queries.shape[1]
    T = kv0.shape[1]
    width = min(t, 512)
    row, specs = attention_specs(width, T, first, kv0.shape[0] // HEAD_DIM // 2)
    size = heads * t * 2 * T
    grads = pl.BlockSpec((HEAD_DIM, T), lambda h, i: (h, 0))
    return pl.pallas_call(
        back_kernel,
        grid=(heads, t // width),
        in_specs=specs + [pl.BlockSpec((1, 1, width), lambda h, i: (h, 0, i)), row],
        out_specs=[row] + [grads] * 4,
        out_shape=[jax.ShapeDtypeStruct(queries.shape, bf16)]
        + [jax.ShapeDtypeStruct((heads * HEAD_DIM, T), d) for d in (f32, f32, bf16, bf16)],
        scratch_shapes=[pltpu.VMEM((4, HEAD_DIM, T), f32)],
        compiler_params=pltpu.CompilerParams(vmem_limit_bytes=48 * 2**20),
        cost_estimate=pl.CostEstimate(
            flops=size * 10 * HEAD_DIM * 4, bytes_accessed=8 * kv0.size, transcendentals=size
        ),
    )(queries, kv0, kv0, kv1, kv1, query_rank, rank0, rank1, log_total, grad)


def shards(
    tokens,
    block_order,
    first_gain,
    first_shift,
    qkv_weight,
    query_value_bias,
    output_weight,
    output_bias,
    second_gain,
    second_shift,
    up_weight,
    up_bias,
    down_weight,
    down_bias,
    cotangent,
):
    R, G = lax.axis_size("row"), lax.axis_size("dp")
    r, c, g = lax.axis_index("row"), lax.axis_index("col"), lax.axis_index("dp")
    low = c == 0
    db, T = tokens.shape
    tq = T // R
    hp = HEADS // R
    W = hp * HEAD_DIM
    E = HEADS * HEAD_DIM - W * R
    X = E // HEAD_DIM
    half = W // 2
    pw = max(half, 2 * E)
    sub = up_weight.shape[1] // R
    GH = G // 2
    hr = db // GH

    def pad(values):
        return jnp.pad(values, ((0, 0), (0, pw - values.shape[1])))

    side = qkv_weight.shape[1] - D
    own_part = cut(qkv_weight, c * side, D, 1)
    own_keys = cut(qkv_weight, (1 - c) * D, side, 1)
    other_keys = swap(own_keys, "col", 1)
    key_part = jnp.concatenate(
        [jnp.where(low, own_keys, other_keys), jnp.where(low, other_keys, own_keys)], 1
    )
    source = jnp.where(g == 3, key_part, own_part)
    extra_keys = jnp.where(low, key_part[:, R * W :], 0)
    extras = pad(jnp.concatenate([own_part[:, R * W :], extra_keys], 1))
    offset = jnp.where(g == 3, c, g & 1) * half
    chunks = [
        jnp.where(g == 2, extras, pad(cut(source, (r ^ k) * W + offset, half, 1)))
        for k in range(R)
    ]
    piece = jnp.concatenate(trade(chunks, "row"), 0)
    x = jnp.concatenate(
        gather_near(tokens, "row", lambda sent: after(sent, piece[D - db :])), 0
    ).astype(f32)
    vectors = jnp.concatenate(
        gather_near(
            jnp.stack([first_gain, first_shift, output_bias, second_gain, second_shift]), "row"
        ),
        1,
    )
    g1, s1, ob, g2, s2 = [vectors[i][:, None] for i in range(5)]

    own_w = jnp.concatenate(settle(spread(piece, "dp"), g), 1)
    other_w = swap(own_w, "col", 1)
    lo, hi = jnp.where(low, own_w, other_w), jnp.where(low, other_w, own_w)
    wqkv = jnp.concatenate([lo, hi], 1)
    HW = W + E
    ex = 2 * pw
    kk = 3 * pw
    end = 4 * pw

    def arrange(main, main_x, extra_k, main_k):
        def fill(values):
            return jnp.pad(values, ((0, pw - values.shape[0]), (0, 0)))

        return [
            fill(main[:half]),
            fill(main[half:]),
            fill(jnp.concatenate([main_x, extra_k], 0)),
            fill(main_k),
        ]

    def bias_rows(values):
        nothing = jnp.zeros((E, 1), f32)
        return arrange(cut(values, r * W, W, 0), values[R * W :], nothing, nothing)

    bias = jnp.concatenate(
        [p for i in (0, 1) for p in bias_rows(query_value_bias[i][:, None])], 0
    )

    block = T * 2 // block_order.shape[1]
    places = (
        block_order.reshape(-1)[:, None] * block + jnp.arange(block, dtype=jnp.int32)[None, :]
    ).reshape(-1)
    own_places = cut(places, c * T, T, 0)
    other_places = cut(places, (1 - c) * T, T, 0)
    rank0, rank1 = own_places[:, None], other_places[:, None]
    query_rank = own_places[None, :]
    extra_rank = cut(query_rank, r * tq, tq, 1)

    normed1, n1, inv1 = norm_forward(x, g1, s1)
    projected = (dot(wqkv, normed1, 0, 0) + bias).astype(bf16)

    def rows_of(at, size):
        return projected[at : at + size]

    queries = jnp.concatenate([rows_of(0, half), rows_of(pw, half)], 0)
    queries_x = cut(rows_of(ex, E), r * tq, tq, 1)
    kv0 = jnp.concatenate(
        [
            rows_of(kk, half),
            rows_of(end + kk, half),
            rows_of(ex + E, E),
            rows_of(end, half),
            rows_of(end + pw, half),
            rows_of(end + ex, E),
        ],
        0,
    )
    kv1 = swap(kv0, "col", 1)
    outx, log_x = attend(queries_x, kv0, kv1, extra_rank, rank0, rank1, hp)
    out, log_main = attend(queries, kv0, kv1, query_rank, rank0, rank1, 0)
    part = jnp.where(
        g < GH,
        cut(up_weight, (g % GH) * hr, hr, 0),
        cut(down_weight, (g % GH) * hr, hr, 0),
    )
    part_o = cut(output_weight, g * (output_weight.shape[0] // G), output_weight.shape[0] // G, 0)
    part = after(part, piece[D - db :])
    pieces = trade([cut(part, (r ^ k) * sub, sub, 1) for k in range(R)], "row")
    piece_o = jnp.concatenate(
        gather_near(after(part_o, piece[D - db :]), "row", lambda v: after(v, kv1)), 1
    )
    part = after(jnp.stack(pieces), kv1)
    which, part_high = (g & GH) != 0, (g & 1) != 0

    def both_weights(values):
        other = swap(values, "dp", GH)
        return jnp.stack(
            [jnp.where(which, other, values), jnp.where(which, values, other)], 0
        )

    def both_halves(values):
        other = swap(values, "dp", 1)
        return jnp.stack(
            [jnp.where(part_high, other, values), jnp.where(part_high, values, other)], -3
        )

    RH = R // 2
    front = both_halves(after(both_weights(part[:RH]), out))
    back = both_weights(after(both_halves(part[RH:]), out))
    own_up, own_dn = [
        plain(jnp.concatenate([front[i], back[i]], 0).reshape(D, sub)) for i in (0, 1)
    ]
    own_o = gather_placed(piece_o, "dp", g, (2, 1), lambda v: after(v, out)).reshape(-1, D)
    other_o = swap(own_o, "col", 1)
    wo = jnp.concatenate([jnp.where(low, own_o, other_o), jnp.where(low, other_o, own_o)], 0)

    def swap_rows(values):
        return swap(values.reshape(R * GH, hr, sub), "col", 1).reshape(D, sub)

    other_up, other_dn = swap_rows(own_up), swap_rows(own_dn)
    own_ub = cut(up_bias, r * sub, sub, 0)
    other_ub = swap(own_ub, "col", 1)[None, :]
    own_ub = own_ub[None, :]

    packed = jnp.concatenate([out, outx.reshape(E // R, T)], 0)
    seen = []

    def watch(values):
        seen.append(values)
        return values

    rows = gather_placed(packed, "row", r, bits(R), watch)
    attended = jnp.concatenate(
        [
            rows[:, :W].reshape(R * W, T),
            rows[:, W:].reshape(R, E, tq).transpose(1, 0, 2).reshape(E, T),
        ],
        0,
    )
    middle = x + dot(wo, attended, 0, 0) + ob
    normed2, n2, inv2 = norm_forward(middle, g2, s2)

    hidden_a, slope_a = gelu_pair(dot(normed2, own_up, 0, 0) + own_ub)
    hidden_b, slope_b = gelu_pair(dot(normed2, other_up, 0, 0) + other_ub)

    upstream = jnp.concatenate(
        gather_near(after(cotangent, seen[0]), "row", lambda sent: after(sent, rows)), 0
    )
    upstream = lax.optimization_barrier(upstream)
    before_a = (dot(upstream, own_dn, 0, 0) * slope_a).astype(bf16)
    before_b = (dot(upstream, other_dn, 0, 0) * slope_b).astype(bf16)
    part2 = dot(own_up, before_a, 1, 1) + dot(other_up, before_b, 1, 1)
    sg_part = jnp.sum(part2 * n2, 1)
    ss_part = jnp.sum(part2, 1)
    back2 = norm_backward(part2, n2, inv2, g2)
    away_up = plain(dot(normed2, before_b, 1, 0).astype(bf16))
    away_dn = plain(dot(upstream, hidden_b, 1, 0).astype(bf16))
    home_up = plain(dot(normed2, before_a, 1, 0))
    home_dn = plain(dot(upstream, hidden_a, 1, 0))
    seen2 = []
    mine = reduce_near(
        [cut(back2, (r ^ k) * tq, tq, 1) for k in range(R)],
        "row",
        lambda piece, bit: jnp.concatenate(
            [piece[(j ^ bit) * db : ((j ^ bit) + 1) * db] for j in range(R)], 0
        ),
        None,
        seen2,
    )
    mine = mine + cut(upstream, r * tq, tq, 1).astype(f32)

    def col_sum(home, away):
        values = home + swap_rows(away).astype(f32)
        values = plain(after(values, seen2[0]).astype(bf16))
        return values.reshape(R, GH, hr, sub)

    down = dot(own_dn, hidden_a, 1, 1) + dot(other_dn, hidden_b, 1, 1)
    down = after(down, seen2[0])
    up_sum, dn_sum = col_sum(home_up, away_up), col_sum(home_dn, away_dn)
    def by_weight(up, dn):
        arrived = swap(jnp.where(which, up, dn).astype(bf16), "dp", GH)
        return jnp.where(which, dn, up).astype(f32) + arrived.astype(f32), arrived

    def by_half(values):
        arrived = swap(
            jnp.where(part_high, values[..., 0, :, :], values[..., 1, :, :]).astype(bf16), "dp", 1
        )
        kept = jnp.where(part_high, values[..., 1, :, :], values[..., 0, :, :])
        return kept.astype(f32) + arrived.astype(f32)

    first, stage = by_weight(up_sum[:RH], dn_sum[:RH])
    second_up, second_dn = by_half(up_sum[RH:]), by_half(dn_sum[RH:])

    branch = mine.astype(bf16)
    ob_part = jnp.sum(branch.astype(f32), 1)
    grad_att = dot(wo, branch, 1, 0).astype(bf16)
    go = jnp.concatenate(
        settle(trade([cut(grad_att, (r ^ k) * W, W, 0) for k in range(R)], "row"), r), 1
    )
    gox = grad_att[R * W :]
    log_main = after(after(log_main, up_sum), dn_sum)
    gqx, *gx = attend_back(
        queries_x, kv0, kv1, extra_rank, rank0, rank1, hp, log_x, gox
    )
    gq, *gm = attend_back(queries, kv0, kv1, query_rank, rank0, rank1, 0, log_main, go)

    down = reduce_near(
        [down[k * db : (k + 1) * db] for k in range(R)],
        "row",
        None,
        lambda sent: after(sent, go),
    )

    away = jnp.concatenate([gm[2], gx[2], gm[3], gx[3]], 0)
    arrived = swap(away, "col", 1)
    gkv = (jnp.concatenate([gm[0], gx[0], gm[1], gx[1]], 0) + arrived.astype(f32)).astype(bf16)
    gqx = lax.dynamic_update_slice_in_dim(jnp.zeros((E, T), bf16), gqx, r * tq, 1)
    gk, gkx, gv, gvx = gkv[:W], gkv[W:HW], gkv[HW : HW + W], gkv[HW + W :]
    grad_p = jnp.concatenate(
        arrange(gq, gqx, gkx, gk[:half]) + arrange(gv, gvx, gkx, gk[half:]), 0
    )
    sums = jnp.sum(grad_p.astype(f32), 1)
    dw = dot(normed1, grad_p, 1, 1)
    lo_w, hi_w = dw[:, :end], dw[:, end:]
    arrived = swap(jnp.where(low, hi_w, lo_w).astype(bf16), "col", 1)
    mine_w = (jnp.where(low, lo_w, hi_w) + arrived.astype(f32)).astype(bf16)
    part1 = dot(wqkv, grad_p, 1, 0)
    fg_part = jnp.sum(part1 * n1, 1)
    fs_part = jnp.sum(part1, 1)
    back1 = norm_backward(part1, n1, inv1, after(g1, arrived))
    back1_low = back1.astype(bf16)

    mine_w = total(
        trade([cut(mine_w, (g ^ k) * pw, pw, 1) for k in range(G)], "dp")
    ).astype(bf16)
    back1 = reduce_near(
        [back1[k * db : (k + 1) * db] for k in range(R)],
        "row",
        None,
        lambda sent: after(sent, mine_w),
    )
    mine_w = jnp.stack(settle(trade(list(mine_w.reshape(R, db, pw)), "row"), r))
    parts = settle(spread(mine_w, "dp"), g)
    ends = total([parts[2][i] for i in range(R)]).astype(bf16)
    mains = [p[:, :half] for i in range(R) for p in (parts[0][i], parts[1][i])]
    keys_own = jnp.stack([parts[3][i][:, :half] for i in range(R)])
    keys_other = swap(keys_own, "col", 1)
    keys_lo = jnp.where(low, keys_own, keys_other)
    keys_hi = jnp.where(low, keys_other, keys_own)
    keys_grad = jnp.concatenate(
        [p for i in range(R) for p in (keys_lo[i], keys_hi[i])] + [ends[:, E : 2 * E]], 1
    )
    main_grad = jnp.concatenate(mains + [ends[:, :E]], 1)
    qkv_weight_grad = jnp.where(
        low,
        jnp.concatenate([main_grad, keys_grad[:, :side]], 1),
        jnp.concatenate([keys_grad[:, D - side :], main_grad], 1),
    ).astype(f32)

    first = by_half(after(first, back1_low))
    second, _ = by_weight(after(second_up, back1_low), second_dn)
    both = jnp.concatenate([first, second], 0).astype(bf16)
    both = settle(trade(list(both), "row"), r)
    wide = R // 2 * sub
    both = jnp.concatenate(both, 1)
    both = jnp.concatenate(
        [
            gather_placed(both[:, :wide], "dp", g, (2, 1), watch),
            gather_placed(both[:, wide:], "dp", g, (1, 2)),
        ],
        2,
    )
    up_weight_grad = both[:GH].reshape(db, -1).astype(f32)
    down_weight_grad = both[GH:].reshape(db, -1).astype(f32)

    branch_rows = jnp.concatenate(
        settle(trade(list(after(branch, back1_low).reshape(R, db, tq)), "row"), r), 1
    )
    result = (middle[:db] + after(down, back1_low) + down_bias[:, None]).astype(bf16)
    input_grad = branch_rows.astype(f32) + back1

    dwo = after(dot(attended, branch_rows, 1, 1), back1_low)
    side_rows = dwo.shape[0] // 2
    lo_o, hi_o = dwo[:side_rows], dwo[side_rows:]
    arrived = swap(jnp.where(low, hi_o, lo_o).astype(bf16), "col", 1)
    mine_o = (jnp.where(low, lo_o, hi_o) + arrived.astype(f32)).astype(bf16)
    mine_o = mine_o.reshape(G, side_rows // G, db)
    mine_o = reduce_placed(mine_o, "dp", g, (1, 2)).astype(bf16)
    output_weight_grad = (
        gather_placed(mine_o, "dp", g, (2, 1)).reshape(side_rows, db).astype(f32)
    )

    rel = jnp.stack([fg_part, fs_part, ob_part, sg_part, ss_part])
    rel = jnp.concatenate(settle(jnp.split(rel, R, 1), r), 1)

    def widen(values, width, start):
        return lax.dynamic_update_slice_in_dim(jnp.zeros((width,), f32), values, start, 0)

    db_part = widen(jnp.sum(cotangent.astype(f32), 1), D, r * db)

    def placed(at):
        main = jnp.concatenate([sums[at : at + half], sums[at + pw : at + pw + half]])
        return jnp.concatenate([widen(main, R * W, r * W), sums[at + ex : at + ex + E]])

    sum_a = jnp.sum(before_a.astype(f32), 0)
    sum_b = jnp.sum(before_b.astype(f32), 0)
    full = up_bias.shape[0]
    ub_part = widen(sum_a, 2 * full, c * full + r * sub) + widen(
        sum_b, 2 * full, (1 - c) * full + r * sub
    )
    small = jnp.concatenate(
        [
            rel,
            db_part[None],
            placed(0)[None],
            placed(end)[None],
            ub_part.reshape(-1, D),
        ],
        0,
    )
    small = after(small, seen[-1])
    for axis in ("col", "row", "dp"):
        k = 1
        while k < lax.axis_size(axis):
            small = small + swap(small, axis, k)
            k *= 2
    return (
        result,
        input_grad,
        small[0],
        small[1],
        qkv_weight_grad,
        small[6:8],
        output_weight_grad,
        small[2],
        small[3],
        small[4],
        up_weight_grad,
        small[8:].reshape(-1),
        down_weight_grad,
        small[5],
    )


def solution(mesh):
    placed = (
        P("row", ("dp", "col")),
        P("dp", None),
        P("row"),
        P("row"),
        P("row", "col"),
        P(),
        P("col", "row"),
        P("row"),
        P("row"),
        P("row"),
        P("row", "col"),
        P("col"),
        P("row", "col"),
        P("row"),
        P("row", ("dp", "col")),
    )
    return jax.shard_map(
        shards,
        mesh=mesh,
        in_specs=placed,
        out_specs=(
            P("row", ("dp", "col")),
            P("row", ("dp", "col")),
            P(),
            P(),
            P("row", "col"),
            P(),
            P("col", "row"),
            P(),
            P(),
            P(),
            P("row", "col"),
            P(),
            P("row", "col"),
            P(),
        ),
        check_vma=False,
    )
```

```python
import jax
import jax.numpy as jnp
from jax import lax
from jax.experimental import pallas as pl
from jax.experimental.layout import Layout, with_layout_constraint
from jax.experimental.pallas import tpu as pltpu
from jax.sharding import PartitionSpec as P

D = 1088
HEADS = 17
HEAD_DIM = 64
FF = 4352
epsilon = 1e-05
f32 = jnp.float32
bf16 = jnp.bfloat16


def gelu_pair(before):
    below = 0.5 + 0.5 * lax.erf(before * 0.5**0.5)
    density = jnp.exp(-0.5 * before * before) * (0.5 / jnp.pi) ** 0.5
    return (before * below).astype(bf16), below + before * density


def dot(left, right, left_dim, right_dim):
    return lax.dot_general(
        left, right, (((left_dim,), (right_dim,)), ((), ())), preferred_element_type=f32
    )


def plain(values):
    return with_layout_constraint(values, Layout(tuple(range(values.ndim))))


def swap(values, axis, k):
    pairs = [(i, i ^ k) for i in range(lax.axis_size(axis))]
    return plain(lax.ppermute(plain(values), axis, pairs))


def spread(values, axis):
    return [values] + [swap(values, axis, k) for k in range(1, lax.axis_size(axis))]


def trade(pieces, axis):
    return [pieces[0]] + [swap(pieces[k], axis, k) for k in range(1, len(pieces))]


def bits(count):
    out = []
    bit = count // 2
    while bit:
        out.append(bit)
        bit //= 2
    return out


def after(values, other):
    first = lax.slice(other, (0,) * other.ndim, (1,) * other.ndim).reshape(())
    return values + (first.astype(f32) * 0.0).astype(values.dtype)


def gather_near(values, axis, hold=None):
    got = {0: values}
    rows = values.shape[0]
    for bit in bits(lax.axis_size(axis)):
        names = sorted(got)
        sent = jnp.concatenate([got[k] for k in names], 0)
        if hold is not None and len(names) > 1:
            sent = hold(sent)
        arrived = swap(sent, axis, bit)
        for i, k in enumerate(names):
            got[k ^ bit] = arrived[i * rows : (i + 1) * rows]
    return [got[k] for k in range(len(got))]


def reduce_near(pieces, axis, regroup=None, hold=None, seen=None):
    left = dict(enumerate(pieces))
    rows = pieces[0].shape[0]
    for bit in bits(len(pieces))[::-1]:
        names = [k for k in sorted(left) if k & bit]
        sent = [left.pop(k) for k in names]
        if regroup is not None:
            sent = [regroup(piece, bit) for piece in sent]
        sent = jnp.concatenate(sent, 0).astype(bf16)
        if hold is not None and len(names) == 1:
            sent = hold(sent)
        arrived = swap(sent, axis, bit)
        if seen is not None:
            seen.append(arrived)
        for i, k in enumerate(names):
            left[k ^ bit] = left[k ^ bit] + arrived[i * rows : (i + 1) * rows].astype(f32)
    return left[0]


def gather_placed(values, axis, index, order, hold=None):
    done = []
    for bit in order:
        if hold is not None and done:
            values = hold(values)
        other = swap(values, axis, bit)
        high = (index & bit) != 0
        values = jnp.stack(
            [jnp.where(high, other, values), jnp.where(high, values, other)],
            sum(1 for b in done if b > bit),
        )
        done.append(bit)
    return values.reshape((-1,) + values.shape[len(done) :])


def reduce_placed(values, axis, index, order, steps=False):
    count = lax.axis_size(axis)
    names = bits(count)
    values = values.reshape((2,) * len(names) + values.shape[1:])
    for bit in order:
        place = names.index(bit)
        zero, one = [lax.index_in_dim(values, i, place, False) for i in (0, 1)]
        high = (index & bit) != 0
        arrived = swap(jnp.where(high, zero, one).astype(bf16), axis, bit)
        values = jnp.where(high, one, zero).astype(f32) + arrived.astype(f32)
        names.remove(bit)
        if steps and bit == order[0]:
            stage = arrived
    return (values, stage) if steps else values


def settle(pieces, index):
    pieces = list(pieces)
    bit = 1
    while bit < len(pieces):
        odd = (index & bit) != 0
        pieces = [jnp.where(odd, pieces[k ^ bit], pieces[k]) for k in range(len(pieces))]
        bit *= 2
    return pieces


def total(pieces):
    out = pieces[0].astype(f32)
    for piece in pieces[1:]:
        out = out + piece.astype(f32)
    return out


def cut(values, start, size, dim):
    return lax.dynamic_slice_in_dim(values, start, size, dim)


def norm_forward(rows, gain, shift):
    average = jnp.sum(rows, 0, keepdims=True) / D
    centered = rows - average
    variance = jnp.sum(centered * centered, 0, keepdims=True) / D
    inverse = lax.rsqrt(variance + epsilon)
    normal = centered * inverse
    return (normal * gain + shift).astype(bf16), normal, inverse


def norm_backward(upstream, normal, inverse, gain):
    scaled = upstream * gain
    first = jnp.sum(scaled, 0, keepdims=True) / D
    second = jnp.sum(scaled * normal, 0, keepdims=True) / D
    return inverse * (scaled - first - normal * second)


SCALE = HEAD_DIM ** (-0.5)


def masked(keys, scaled, key_rank, query_rank):
    scores = dot(keys, scaled, 0, 0)
    return jnp.where(key_rank <= query_rank, scores, -1e30)


def attend_kernel(q, k0, v0, k1, v1, query_rank, rank0, rank1, out, log_total):
    scaled = q[...] * jnp.asarray(SCALE, bf16)
    query = query_rank[...]
    s0 = masked(k0[...], scaled, rank0[...], query)
    s1 = masked(k1[...], scaled, rank1[...], query)
    largest = jnp.maximum(jnp.max(s0, 0, keepdims=True), jnp.max(s1, 0, keepdims=True))
    p0 = jnp.exp(s0 - largest)
    p1 = jnp.exp(s1 - largest)
    totals = jnp.sum(p0, 0, keepdims=True) + jnp.sum(p1, 0, keepdims=True)
    got = dot(v0[...], p0.astype(bf16), 1, 0) + dot(v1[...], p1.astype(bf16), 1, 0)
    out[...] = (got / totals).astype(bf16)
    log_total[...] = (largest + jnp.log(totals))[None]


def back_kernel(
    q, k0, v0, k1, v1, query_rank, rank0, rank1, log_total, grad, gq, gk0, gv0, gk1, gv1, sums
):
    step = pl.program_id(1)

    @pl.when(step == 0)
    def _():
        sums[...] = jnp.zeros_like(sums)

    scaled = q[...] * jnp.asarray(SCALE, bf16)
    query = query_rank[...]
    shift = log_total[...][0]
    g = grad[...]
    p0 = jnp.exp(masked(k0[...], scaled, rank0[...], query) - shift)
    p1 = jnp.exp(masked(k1[...], scaled, rank1[...], query) - shift)
    w0 = dot(v0[...], g, 0, 0)
    w1 = dot(v1[...], g, 0, 0)
    inner = jnp.sum(p0 * w0, 0, keepdims=True) + jnp.sum(p1 * w1, 0, keepdims=True)
    d0 = (p0 * (w0 - inner)).astype(bf16)
    d1 = (p1 * (w1 - inner)).astype(bf16)
    gq[...] = ((dot(k0[...], d0, 1, 0) + dot(k1[...], d1, 1, 0)) * SCALE).astype(gq.dtype)
    sums[0] += dot(scaled, d0, 1, 1)
    sums[1] += dot(g, p0.astype(bf16), 1, 1)
    sums[2] += dot(scaled, d1, 1, 1)
    sums[3] += dot(g, p1.astype(bf16), 1, 1)

    @pl.when(step == pl.num_programs(1) - 1)
    def _():
        gk0[...] = sums[0].astype(gk0.dtype)
        gv0[...] = sums[1].astype(gv0.dtype)
        gk1[...] = sums[2].astype(gk1.dtype)
        gv1[...] = sums[3].astype(gv1.dtype)


def attention_specs(width, T, first, all_heads):
    def key_spec(at):
        return pl.BlockSpec((HEAD_DIM, T), lambda h, i: (at + h, 0))

    row = pl.BlockSpec((HEAD_DIM, width), lambda h, i: (h, i))
    ranks = [pl.BlockSpec((1, width), lambda h, i: (0, i))] + [
        pl.BlockSpec((T, 1), lambda h, i: (0, 0))
    ] * 2
    pair = [key_spec(first), key_spec(all_heads + first)]
    return row, [row] + pair + pair + ranks


def attend(queries, kv0, kv1, query_rank, rank0, rank1, first):
    heads, t = queries.shape[0] // HEAD_DIM, queries.shape[1]
    T = kv0.shape[1]
    width = min(t, 512)
    row, specs = attention_specs(width, T, first, kv0.shape[0] // HEAD_DIM // 2)
    size = heads * t * 2 * T
    return pl.pallas_call(
        attend_kernel,
        grid=(heads, t // width),
        in_specs=specs,
        out_specs=[row, pl.BlockSpec((1, 1, width), lambda h, i: (h, 0, i))],
        out_shape=[
            jax.ShapeDtypeStruct(queries.shape, bf16),
            jax.ShapeDtypeStruct((heads, 1, t), f32),
        ],
        compiler_params=pltpu.CompilerParams(vmem_limit_bytes=40 * 2**20),
        cost_estimate=pl.CostEstimate(
            flops=size * 4 * HEAD_DIM * 4, bytes_accessed=4 * kv0.size, transcendentals=size
        ),
    )(queries, kv0, kv0, kv1, kv1, query_rank, rank0, rank1)


def attend_back(queries, kv0, kv1, query_rank, rank0, rank1, first, log_total, grad):
    heads, t = queries.shape[0] // HEAD_DIM, queries.shape[1]
    T = kv0.shape[1]
    width = min(t, 512)
    row, specs = attention_specs(width, T, first, kv0.shape[0] // HEAD_DIM // 2)
    size = heads * t * 2 * T
    grads = pl.BlockSpec((HEAD_DIM, T), lambda h, i: (h, 0))
    return pl.pallas_call(
        back_kernel,
        grid=(heads, t // width),
        in_specs=specs + [pl.BlockSpec((1, 1, width), lambda h, i: (h, 0, i)), row],
        out_specs=[row] + [grads] * 4,
        out_shape=[jax.ShapeDtypeStruct(queries.shape, bf16)]
        + [jax.ShapeDtypeStruct((heads * HEAD_DIM, T), d) for d in (f32, f32, bf16, bf16)],
        scratch_shapes=[pltpu.VMEM((4, HEAD_DIM, T), f32)],
        compiler_params=pltpu.CompilerParams(vmem_limit_bytes=48 * 2**20),
        cost_estimate=pl.CostEstimate(
            flops=size * 10 * HEAD_DIM * 4, bytes_accessed=8 * kv0.size, transcendentals=size
        ),
    )(queries, kv0, kv0, kv1, kv1, query_rank, rank0, rank1, log_total, grad)


def shards(
    tokens,
    block_order,
    first_gain,
    first_shift,
    qkv_weight,
    query_value_bias,
    output_weight,
    output_bias,
    second_gain,
    second_shift,
    up_weight,
    up_bias,
    down_weight,
    down_bias,
    cotangent,
):
    R, G = lax.axis_size("row"), lax.axis_size("dp")
    r, c, g = lax.axis_index("row"), lax.axis_index("col"), lax.axis_index("dp")
    low = c == 0
    db, T = tokens.shape
    tq = T // R
    hp = HEADS // R
    W = hp * HEAD_DIM
    E = HEADS * HEAD_DIM - W * R
    X = E // HEAD_DIM
    half = W // 2
    pw = max(half, 2 * E)
    sub = up_weight.shape[1] // R
    GH = G // 2
    hr = db // GH

    def pad(values):
        return jnp.pad(values, ((0, 0), (0, pw - values.shape[1])))

    side = qkv_weight.shape[1] - D
    own_part = cut(qkv_weight, c * side, D, 1)
    own_keys = cut(qkv_weight, (1 - c) * D, side, 1)
    other_keys = swap(own_keys, "col", 1)
    key_part = jnp.concatenate(
        [jnp.where(low, own_keys, other_keys), jnp.where(low, other_keys, own_keys)], 1
    )
    source = jnp.where(g == 3, key_part, own_part)
    extra_keys = jnp.where(low, key_part[:, R * W :], 0)
    extras = pad(jnp.concatenate([own_part[:, R * W :], extra_keys], 1))
    offset = jnp.where(g == 3, c, g & 1) * half
    chunks = [
        jnp.where(g == 2, extras, pad(cut(source, (r ^ k) * W + offset, half, 1)))
        for k in range(R)
    ]
    piece = jnp.concatenate(trade(chunks, "row"), 0)
    x = jnp.concatenate(
        gather_near(tokens, "row", lambda sent: after(sent, piece[D - db :])), 0
    ).astype(f32)
    vectors = jnp.concatenate(
        gather_near(
            jnp.stack([first_gain, first_shift, output_bias, second_gain, second_shift]), "row"
        ),
        1,
    )
    g1, s1, ob, g2, s2 = [vectors[i][:, None] for i in range(5)]

    own_w = jnp.concatenate(settle(spread(piece, "dp"), g), 1)
    other_w = swap(own_w, "col", 1)
    lo, hi = jnp.where(low, own_w, other_w), jnp.where(low, other_w, own_w)
    wqkv = jnp.concatenate([lo, hi], 1)
    HW = W + E
    ex = 2 * pw
    kk = 3 * pw
    end = 4 * pw

    def arrange(main, main_x, extra_k, main_k):
        def fill(values):
            return jnp.pad(values, ((0, pw - values.shape[0]), (0, 0)))

        return [
            fill(main[:half]),
            fill(main[half:]),
            fill(jnp.concatenate([main_x, extra_k], 0)),
            fill(main_k),
        ]

    def bias_rows(values):
        nothing = jnp.zeros((E, 1), f32)
        return arrange(cut(values, r * W, W, 0), values[R * W :], nothing, nothing)

    bias = jnp.concatenate(
        [p for i in (0, 1) for p in bias_rows(query_value_bias[i][:, None])], 0
    )

    block = T * 2 // block_order.shape[1]
    places = (
        block_order.reshape(-1)[:, None] * block + jnp.arange(block, dtype=jnp.int32)[None, :]
    ).reshape(-1)
    own_places = cut(places, c * T, T, 0)
    other_places = cut(places, (1 - c) * T, T, 0)
    rank0, rank1 = own_places[:, None], other_places[:, None]
    query_rank = own_places[None, :]
    extra_rank = cut(query_rank, r * tq, tq, 1)

    normed1, n1, inv1 = norm_forward(x, g1, s1)
    projected = (dot(wqkv, normed1, 0, 0) + bias).astype(bf16)

    def rows_of(at, size):
        return projected[at : at + size]

    queries = jnp.concatenate([rows_of(0, half), rows_of(pw, half)], 0)
    queries_x = cut(rows_of(ex, E), r * tq, tq, 1)
    kv0 = jnp.concatenate(
        [
            rows_of(kk, half),
            rows_of(end + kk, half),
            rows_of(ex + E, E),
            rows_of(end, half),
            rows_of(end + pw, half),
            rows_of(end + ex, E),
        ],
        0,
    )
    kv1 = swap(kv0, "col", 1)
    outx, log_x = attend(queries_x, kv0, kv1, extra_rank, rank0, rank1, hp)
    out, log_main = attend(queries, kv0, kv1, query_rank, rank0, rank1, 0)
    part = jnp.where(
        g < GH,
        cut(up_weight, (g % GH) * hr, hr, 0),
        cut(down_weight, (g % GH) * hr, hr, 0),
    )
    part_o = cut(output_weight, g * (output_weight.shape[0] // G), output_weight.shape[0] // G, 0)
    part = after(part, piece[D - db :])
    pieces = trade([cut(part, (r ^ k) * sub, sub, 1) for k in range(R)], "row")
    piece_o = jnp.concatenate(
        gather_near(after(part_o, piece[D - db :]), "row", lambda v: after(v, kv1)), 1
    )
    part = after(jnp.stack(pieces), kv1)
    which, part_high = (g & GH) != 0, (g & 1) != 0

    def both_weights(values):
        other = swap(values, "dp", GH)
        return jnp.stack(
            [jnp.where(which, other, values), jnp.where(which, values, other)], 0
        )

    def both_halves(values):
        other = swap(values, "dp", 1)
        return jnp.stack(
            [jnp.where(part_high, other, values), jnp.where(part_high, values, other)], -3
        )

    RH = R // 2
    front = both_halves(after(both_weights(part[:RH]), out))
    back = both_weights(after(both_halves(part[RH:]), out))
    own_up, own_dn = [
        plain(jnp.concatenate([front[i], back[i]], 0).reshape(D, sub)) for i in (0, 1)
    ]
    own_o = gather_placed(piece_o, "dp", g, (2, 1), lambda v: after(v, out)).reshape(-1, D)
    other_o = swap(own_o, "col", 1)
    wo = jnp.concatenate([jnp.where(low, own_o, other_o), jnp.where(low, other_o, own_o)], 0)

    def swap_rows(values):
        return swap(values.reshape(R * GH, hr, sub), "col", 1).reshape(D, sub)

    other_up, other_dn = swap_rows(own_up), swap_rows(own_dn)
    own_ub = cut(up_bias, r * sub, sub, 0)
    other_ub = swap(own_ub, "col", 1)[None, :]
    own_ub = own_ub[None, :]

    packed = jnp.concatenate([out, outx.reshape(E // R, T)], 0)
    seen = []

    def watch(values):
        seen.append(values)
        return values

    rows = gather_placed(packed, "row", r, bits(R), watch)
    attended = jnp.concatenate(
        [
            rows[:, :W].reshape(R * W, T),
            rows[:, W:].reshape(R, E, tq).transpose(1, 0, 2).reshape(E, T),
        ],
        0,
    )
    middle = x + dot(wo, attended, 0, 0) + ob
    normed2, n2, inv2 = norm_forward(middle, g2, s2)

    hidden_a, slope_a = gelu_pair(dot(normed2, own_up, 0, 0) + own_ub)
    hidden_b, slope_b = gelu_pair(dot(normed2, other_up, 0, 0) + other_ub)

    upstream = jnp.concatenate(
        gather_near(after(cotangent, seen[0]), "row", lambda sent: after(sent, rows)), 0
    )
    upstream = lax.optimization_barrier(upstream)
    before_a = (dot(upstream, own_dn, 0, 0) * slope_a).astype(bf16)
    before_b = (dot(upstream, other_dn, 0, 0) * slope_b).astype(bf16)
    part2 = dot(own_up, before_a, 1, 1) + dot(other_up, before_b, 1, 1)
    sg_part = jnp.sum(part2 * n2, 1)
    ss_part = jnp.sum(part2, 1)
    back2 = norm_backward(part2, n2, inv2, g2)
    away_up = plain(dot(normed2, before_b, 1, 0).astype(bf16))
    away_dn = plain(dot(upstream, hidden_b, 1, 0).astype(bf16))
    home_up = plain(dot(normed2, before_a, 1, 0))
    home_dn = plain(dot(upstream, hidden_a, 1, 0))
    seen2 = []
    mine = reduce_near(
        [cut(back2, (r ^ k) * tq, tq, 1) for k in range(R)],
        "row",
        lambda piece, bit: jnp.concatenate(
            [piece[(j ^ bit) * db : ((j ^ bit) + 1) * db] for j in range(R)], 0
        ),
        None,
        seen2,
    )
    mine = mine + cut(upstream, r * tq, tq, 1).astype(f32)

    def col_sum(home, away):
        values = home + swap_rows(away).astype(f32)
        values = plain(after(values, seen2[0]).astype(bf16))
        return values.reshape(R, GH, hr, sub)

    down = dot(own_dn, hidden_a, 1, 1) + dot(other_dn, hidden_b, 1, 1)
    down = after(down, seen2[0])
    up_sum, dn_sum = col_sum(home_up, away_up), col_sum(home_dn, away_dn)
    def by_weight(up, dn):
        arrived = swap(jnp.where(which, up, dn).astype(bf16), "dp", GH)
        return jnp.where(which, dn, up).astype(f32) + arrived.astype(f32), arrived

    def by_half(values):
        arrived = swap(
            jnp.where(part_high, values[..., 0, :, :], values[..., 1, :, :]).astype(bf16), "dp", 1
        )
        kept = jnp.where(part_high, values[..., 1, :, :], values[..., 0, :, :])
        return kept.astype(f32) + arrived.astype(f32)

    first, stage = by_weight(up_sum[:RH], dn_sum[:RH])
    second_up, second_dn = by_half(up_sum[RH:]), by_half(dn_sum[RH:])

    branch = mine.astype(bf16)
    ob_part = jnp.sum(branch.astype(f32), 1)
    grad_att = dot(wo, branch, 1, 0).astype(bf16)
    go = jnp.concatenate(
        settle(trade([cut(grad_att, (r ^ k) * W, W, 0) for k in range(R)], "row"), r), 1
    )
    gox = grad_att[R * W :]
    log_main = after(after(log_main, up_sum), dn_sum)
    gqx, *gx = attend_back(
        queries_x, kv0, kv1, extra_rank, rank0, rank1, hp, log_x, gox
    )
    gq, *gm = attend_back(queries, kv0, kv1, query_rank, rank0, rank1, 0, log_main, go)

    down = reduce_near(
        [down[k * db : (k + 1) * db] for k in range(R)],
        "row",
        None,
        lambda sent: after(sent, go),
    )

    away = jnp.concatenate([gm[2], gx[2], gm[3], gx[3]], 0)
    arrived = swap(away, "col", 1)
    gkv = (jnp.concatenate([gm[0], gx[0], gm[1], gx[1]], 0) + arrived.astype(f32)).astype(bf16)
    gqx = lax.dynamic_update_slice_in_dim(jnp.zeros((E, T), bf16), gqx, r * tq, 1)
    gk, gkx, gv, gvx = gkv[:W], gkv[W:HW], gkv[HW : HW + W], gkv[HW + W :]
    grad_p = jnp.concatenate(
        arrange(gq, gqx, gkx, gk[:half]) + arrange(gv, gvx, gkx, gk[half:]), 0
    )
    sums = jnp.sum(grad_p.astype(f32), 1)
    dw = dot(normed1, grad_p, 1, 1)
    lo_w, hi_w = dw[:, :end], dw[:, end:]
    arrived = swap(jnp.where(low, hi_w, lo_w).astype(bf16), "col", 1)
    mine_w = (jnp.where(low, lo_w, hi_w) + arrived.astype(f32)).astype(bf16)
    part1 = dot(wqkv, grad_p, 1, 0)
    fg_part = jnp.sum(part1 * n1, 1)
    fs_part = jnp.sum(part1, 1)
    back1 = norm_backward(part1, n1, inv1, after(g1, arrived))
    back1_low = back1.astype(bf16)

    mine_w = total(
        trade([cut(mine_w, (g ^ k) * pw, pw, 1) for k in range(G)], "dp")
    ).astype(bf16)
    back1 = reduce_near(
        [back1[k * db : (k + 1) * db] for k in range(R)],
        "row",
        None,
        lambda sent: after(sent, mine_w),
    )
    mine_w = jnp.stack(settle(trade(list(mine_w.reshape(R, db, pw)), "row"), r))
    parts = settle(spread(mine_w, "dp"), g)
    ends = total([parts[2][i] for i in range(R)]).astype(bf16)
    mains = [p[:, :half] for i in range(R) for p in (parts[0][i], parts[1][i])]
    keys_own = jnp.stack([parts[3][i][:, :half] for i in range(R)])
    keys_other = swap(keys_own, "col", 1)
    keys_lo = jnp.where(low, keys_own, keys_other)
    keys_hi = jnp.where(low, keys_other, keys_own)
    keys_grad = jnp.concatenate(
        [p for i in range(R) for p in (keys_lo[i], keys_hi[i])] + [ends[:, E : 2 * E]], 1
    )
    main_grad = jnp.concatenate(mains + [ends[:, :E]], 1)
    qkv_weight_grad = jnp.where(
        low,
        jnp.concatenate([main_grad, keys_grad[:, :side]], 1),
        jnp.concatenate([keys_grad[:, D - side :], main_grad], 1),
    ).astype(f32)

    first = by_half(after(first, back1_low))
    second, _ = by_weight(after(second_up, back1_low), second_dn)
    both = jnp.concatenate([first, second], 0).astype(bf16)
    both = settle(trade(list(both), "row"), r)
    wide = R // 2 * sub
    both = jnp.concatenate(both, 1)
    both = jnp.concatenate(
        [
            gather_placed(both[:, :wide], "dp", g, (2, 1), watch),
            gather_placed(both[:, wide:], "dp", g, (1, 2)),
        ],
        2,
    )
    up_weight_grad = both[:GH].reshape(db, -1).astype(f32)
    down_weight_grad = both[GH:].reshape(db, -1).astype(f32)

    branch_rows = jnp.concatenate(
        settle(trade(list(after(branch, back1_low).reshape(R, db, tq)), "row"), r), 1
    )
    result = (middle[:db] + after(down, back1_low) + down_bias[:, None]).astype(bf16)
    input_grad = branch_rows.astype(f32) + back1

    dwo = after(dot(attended, branch_rows, 1, 1), mine_w[0])
    side_rows = dwo.shape[0] // 2
    lo_o, hi_o = dwo[:side_rows], dwo[side_rows:]
    arrived = swap(jnp.where(low, hi_o, lo_o).astype(bf16), "col", 1)
    mine_o = (jnp.where(low, lo_o, hi_o) + arrived.astype(f32)).astype(bf16)
    mine_o = mine_o.reshape(G, side_rows // G, db)
    mine_o = reduce_placed(mine_o, "dp", g, (1, 2)).astype(bf16)
    output_weight_grad = (
        gather_placed(mine_o, "dp", g, (2, 1)).reshape(side_rows, db).astype(f32)
    )

    rel = jnp.stack([fg_part, fs_part, ob_part, sg_part, ss_part])
    rel = jnp.concatenate(settle(jnp.split(rel, R, 1), r), 1)

    def widen(values, width, start):
        return lax.dynamic_update_slice_in_dim(jnp.zeros((width,), f32), values, start, 0)

    db_part = widen(jnp.sum(cotangent.astype(f32), 1), D, r * db)

    def placed(at):
        main = jnp.concatenate([sums[at : at + half], sums[at + pw : at + pw + half]])
        return jnp.concatenate([widen(main, R * W, r * W), sums[at + ex : at + ex + E]])

    sum_a = jnp.sum(before_a.astype(f32), 0)
    sum_b = jnp.sum(before_b.astype(f32), 0)
    full = up_bias.shape[0]
    ub_part = widen(sum_a, 2 * full, c * full + r * sub) + widen(
        sum_b, 2 * full, (1 - c) * full + r * sub
    )
    small = jnp.concatenate(
        [
            rel,
            db_part[None],
            placed(0)[None],
            placed(end)[None],
            ub_part.reshape(-1, D),
        ],
        0,
    )
    small = after(small, seen[-1])
    for axis in ("col", "row", "dp"):
        k = 1
        while k < lax.axis_size(axis):
            small = small + swap(small, axis, k)
            k *= 2
    return (
        result,
        input_grad,
        small[0],
        small[1],
        qkv_weight_grad,
        small[6:8],
        output_weight_grad,
        small[2],
        small[3],
        small[4],
        up_weight_grad,
        small[8:].reshape(-1),
        down_weight_grad,
        small[5],
    )


def solution(mesh):
    placed = (
        P("row", ("dp", "col")),
        P("dp", None),
        P("row"),
        P("row"),
        P("row", "col"),
        P(),
        P("col", "row"),
        P("row"),
        P("row"),
        P("row"),
        P("row", "col"),
        P("col"),
        P("row", "col"),
        P("row"),
        P("row", ("dp", "col")),
    )
    return jax.shard_map(
        shards,
        mesh=mesh,
        in_specs=placed,
        out_specs=(
            P("row", ("dp", "col")),
            P("row", ("dp", "col")),
            P(),
            P(),
            P("row", "col"),
            P(),
            P("col", "row"),
            P(),
            P(),
            P(),
            P("row", "col"),
            P(),
            P("row", "col"),
            P(),
        ),
        check_vma=False,
    )
```
